32 devices in a mesh: slab: 8 (over z, x), energy: 4 (over y, core).
Axes of the slice: x: 2, y: 2, z: 4, core: 2. Of those that a mesh axis runs over, the one named last changes fastest.
Arguments:
- green_lesser: bfloat16 [2, 8, 32, 256, 256], P(None, 'energy', 'slab'), may hold values from -4 to 4
- screened_lesser: bfloat16 [2, 8, 32, 256, 256], P(None, 'energy', 'slab'), may hold values from -4 to 4
- green_retarded: bfloat16 [2, 8, 32, 256, 256], P(None, 'energy', 'slab'), may hold values from -1 to 1
- coupling: bfloat16 [2, 32, 256, 256], P(None, 'slab'), may hold values from -1 to 1
Outputs:
- connected_lesser: float32 [2, 8, 32, 256, 256], P(None, 'energy', 'slab')
The draws below stay inside these ranges and needn't reach their ends.
All inputs are finite; a program needn't handle non-finite values.
Results may differ from the reference program's by a relative error of at most 0.004.
Values may be sent and summed in bfloat16 or wider, within the bound.
No kernel may reach another device: no remote copies, remote signals or barrier semaphores. Data moves between devices by JAX's collectives and lax.ppermute only.
A program may use at most 128 MiB of HBM per device.

```python
import math
import jax
import jax.numpy as jnp
from jax import lax

NORB = 256
SLABS = 32
ENERGIES = 8


def shuffled(single):
    return jax.random.permutation(single, NORB)


def unitary_blocks(key, leading, factor, noise_level):
    blocks_total = math.prod(leading)
    subkeys = jax.random.split(key, 5)
    row_order = jax.vmap(shuffled)(jax.random.split(subkeys[0], blocks_total)).astype(jnp.int32)
    column_order = jax.vmap(shuffled)(jax.random.split(subkeys[1], blocks_total)).astype(jnp.int32)
    row_phase = jax.random.uniform(subkeys[2], (blocks_total, NORB), jnp.float32, -math.pi, math.pi)
    column_phase = jax.random.uniform(subkeys[3], (blocks_total, NORB), jnp.float32, -math.pi, math.pi)
    product_index = row_order[:, :, None] * column_order[:, None, :] % NORB
    angles = row_phase[:, :, None] + column_phase[:, None, :] + 2.0 * math.pi / NORB * product_index.astype(jnp.float32)
    spread = noise_level / math.sqrt(2.0 * NORB)
    full_shape = (2, blocks_total, NORB, NORB)
    disorder = jax.random.truncated_normal(subkeys[4], -4.0, 4.0, full_shape, jnp.float32) * spread
    unitary_part = jnp.stack([jnp.cos(angles), jnp.sin(angles)]) / math.sqrt(NORB)
    result = factor * (unitary_part + disorder)
    return result.reshape((2,) + tuple(leading) + (NORB, NORB))


def draw_green_retarded(key, part):
    return unitary_blocks(jax.random.fold_in(key, 101), (ENERGIES, SLABS), 0.98, 0.2).astype(jnp.bfloat16)


def draw_coupling(key, part):
    return unitary_blocks(jax.random.fold_in(key, 202), (SLABS,), 0.975, 0.2).astype(jnp.bfloat16)


def shard_levels(key, extent, pieces, low, top_value):
    gain, own = 1.0, jax.random.fold_in(key, 6)
    for dim, shards_of in pieces:
        steps = jnp.exp(jax.random.uniform(jax.random.fold_in(own, dim), (shards_of,), jnp.float32, low / len(pieces), top_value / len(pieces)))
        gain = gain * jnp.repeat(steps, extent[dim] // shards_of).reshape([-1 if axis == dim else 1 for axis in range(len(extent))])
    return gain


def noise(stream_key, shape, scale, reach, cuts=(), held_as=jnp.bfloat16):
    values = jax.random.normal(stream_key, shape, jnp.float32) * scale
    if len(cuts) > 0:
        values = shard_levels(stream_key, shape, cuts, -0.22, 0.18) * values
    return jnp.clip(values, min=-reach, max=reach).astype(held_as)


def setup_inputs(seed: int = 0) -> dict:
    keys = jax.random.split(jax.random.key(seed), 5)
    green_lesser = noise(keys[0], (2, ENERGIES, SLABS, NORB, NORB), 1.0, 4.0, ((1, 4), (2, 8)))
    screened_lesser = noise(keys[1], (2, ENERGIES, SLABS, NORB, NORB), 1.0, 4.0, ((1, 4), (2, 8)))
    green_retarded = draw_green_retarded(jax.random.fold_in(keys[4], 71), 0)
    coupling = draw_coupling(jax.random.fold_in(keys[4], 71), 0)
    return {"green_lesser": green_lesser, "screened_lesser": screened_lesser, "green_retarded": green_retarded, "coupling": coupling}


def convolve_energy(green, screen):
    points = green.shape[1]
    middle = points // 2
    widths = [(0, 0)] * green.ndim
    widths[1] = (points, points)
    padded = jnp.pad(green.astype(jnp.float32), widths)
    screen_wide = screen.astype(jnp.float32)

    def add_offset(offset, totals):
        start = (points + middle - offset).astype(jnp.int32)
        shifted = lax.dynamic_slice_in_dim(padded, start, points, 1)
        weight = lax.dynamic_slice_in_dim(screen_wide, offset.astype(jnp.int32), 1, 1)
        real_part = totals[0] + shifted[0] * weight[0] - shifted[1] * weight[1]
        imag_part = totals[1] + shifted[0] * weight[1] + shifted[1] * weight[0]
        return (real_part, imag_part)

    blank_sum = jnp.zeros(green.shape[1:], jnp.float32)
    totals = lax.fori_loop(0, points, add_offset, (blank_sum, blank_sum))
    return jnp.stack([-totals[1] / points, totals[0] / points]).astype(jnp.bfloat16)


def precise(first, second):
    return jnp.dot(first, second, precision=lax.Precision.HIGHEST, preferred_element_type=jnp.float32)


def lowdot(first, second):
    return jnp.dot(first, second, preferred_element_type=jnp.float32)


def congruence(kernel, state, source):
    inner_re = precise(kernel[0], state[0]) - precise(kernel[1], state[1])
    inner_im = precise(kernel[0], state[1]) + precise(kernel[1], state[0])
    outer_re = precise(inner_re, kernel[0].T) + precise(inner_im, kernel[1].T)
    outer_im = precise(inner_im, kernel[0].T) - precise(inner_re, kernel[1].T)
    return (outer_re + source[0], outer_im + source[1])


def reference(green_lesser, screened_lesser, green_retarded, coupling):
    lesser_slabs = jnp.moveaxis(green_lesser, 2, 0)
    screen_slabs = jnp.moveaxis(screened_lesser, 2, 0)

    def convolve_slab(pair):
        return convolve_energy(pair[0], pair[1])

    sigma = lax.map(convolve_slab, (lesser_slabs, screen_slabs))
    sigma_energy = jnp.moveaxis(sigma, 2, 0)
    green_energy = jnp.moveaxis(green_retarded, (1, 2), (0, 1))
    coupling_slabs = jnp.moveaxis(coupling, 1, 0)

    def sweep(pair):
        greens, sigmas = pair

        def advance(state, item):
            green, sigma_block, link = item
            kernel_re = lowdot(green[0], link[0]) - lowdot(green[1], link[1])
            kernel_im = lowdot(green[0], link[1]) + lowdot(green[1], link[0])
            mixed_re = (lowdot(green[0], sigma_block[0]) - lowdot(green[1], sigma_block[1])).astype(jnp.bfloat16)
            mixed_im = (lowdot(green[0], sigma_block[1]) + lowdot(green[1], sigma_block[0])).astype(jnp.bfloat16)
            source_re = lowdot(mixed_re, green[0].T) + lowdot(mixed_im, green[1].T)
            source_im = lowdot(mixed_im, green[0].T) - lowdot(mixed_re, green[1].T)
            updated = congruence((kernel_re, kernel_im), state, (source_re, source_im))
            return updated, jnp.stack(updated)

        blank_block = jnp.zeros((NORB, NORB), jnp.float32)
        final_state, states = lax.scan(advance, (blank_block, blank_block), (greens, sigmas, coupling_slabs))
        return states

    result = lax.map(sweep, (green_energy, sigma_energy))
    return jnp.moveaxis(result, 2, 0)
```

```python
import functools

import jax
import jax.numpy as jnp
from jax import lax
from jax.experimental import pallas as pl
from jax.experimental.pallas import tpu as pltpu
from jax.sharding import PartitionSpec as P

BF16 = jnp.bfloat16
F32 = jnp.float32
VMEM_LIMIT = 24 * 1024 * 1024


def params():
    return pltpu.CompilerParams(vmem_limit_bytes=VMEM_LIMIT)


def cost(products, order, nbytes):
    return pl.CostEstimate(
        flops=2 * products * order**3, bytes_accessed=nbytes, transcendentals=0
    )


def split(value):
    high = value.astype(BF16)
    low = (value - high.astype(F32)).astype(BF16)
    return high, low


def panel(re, im):
    return jnp.concatenate(
        [jnp.concatenate([re, im], axis=1), jnp.concatenate([-im, re], axis=1)], axis=0
    )


def dot(left, right):
    return lax.dot_general(left, right, (((1,), (0,)), ((), ())), preferred_element_type=F32)


def dot_nt(left, right):
    return lax.dot_general(left, right, (((1,), (1,)), ((), ())), preferred_element_type=F32)


def times_wide(a_high, a_low, x):
    order = x.shape[0]
    x_high, x_low = split(x)
    xh = panel(x_high[:, :order], x_high[:, order:])
    xl = panel(x_low[:, :order], x_low[:, order:])
    left = jnp.concatenate([a_high, a_high, a_low], axis=1)
    return dot(left, jnp.concatenate([xh, xl, xh], axis=0))


def times_narrow(a_high, a_low, re, im):
    xp = panel(re, im)
    left = jnp.concatenate([a_high, a_low], axis=1)
    return dot(left, jnp.concatenate([xp, xp], axis=0))


def times_adjoint(y, t_high, t_low):
    order = y.shape[0]
    y_high, y_low = split(y)
    th = panel(t_high[:, :order], t_high[:, order:])
    tl = panel(t_low[:, :order], t_low[:, order:])
    left = jnp.concatenate([y_high, y_low, y_high], axis=1)
    return dot_nt(left, jnp.concatenate([th, th, tl], axis=1))


def panels(ref):
    return ref[0], ref[1]


def store_map(ref, value):
    high, low = split(value)
    ref[0] = high
    ref[1] = low


def maps_body(g_ref, c_ref, k_ref, p_ref, carry):
    left = jnp.concatenate([g_ref[0], g_ref[1]], axis=1)
    value = dot(left, panel(c_ref[0], c_ref[1]))
    store_map(k_ref, value)

    @pl.when(pl.program_id(1) == 0)
    def _():
        carry[...] = value

    @pl.when(pl.program_id(1) > 0)
    def _():
        high, low = panels(k_ref)
        carry[...] = times_wide(high, low, carry[...])

    store_map(p_ref, carry[...])


def build_maps(green, coupling):
    _, energies, slabs, order, _ = green.shape
    shape = jax.ShapeDtypeStruct((energies, slabs, 2, order, 2 * order), BF16)
    out_spec = pl.BlockSpec((None, None, 2, order, 2 * order), lambda e, s: (e, s, 0, 0, 0))
    return pl.pallas_call(
        maps_body,
        grid=(energies, slabs),
        in_specs=[
            pl.BlockSpec((2, None, None, order, order), lambda e, s: (0, e, s, 0, 0)),
            pl.BlockSpec((2, None, order, order), lambda e, s: (0, s, 0, 0)),
        ],
        out_specs=[out_spec, out_spec],
        out_shape=[shape, shape],
        scratch_shapes=[pltpu.VMEM((order, 2 * order), F32)],
        compiler_params=params(),
        cost_estimate=cost(16 * energies * slabs, order, 12 * green.size),
        name="maps",
    )(green, coupling)


def map_product_body(a_ref, b_ref, o_ref):
    high, low = panels(a_ref)
    value = times_wide(high, low, b_ref[0].astype(F32) + b_ref[1].astype(F32))
    store_map(o_ref, value)


def map_product(first, second):
    energies, slabs, _, order, _ = first.shape
    spec = pl.BlockSpec((None, None, 2, order, 2 * order), lambda e, s: (e, s, 0, 0, 0))
    return pl.pallas_call(
        map_product_body,
        grid=(energies, slabs),
        in_specs=[spec, pl.BlockSpec((None, 2, order, 2 * order), lambda e, s: (e, 0, 0, 0))],
        out_specs=spec,
        out_shape=jax.ShapeDtypeStruct(first.shape, BF16),
        compiler_params=params(),
        cost_estimate=cost(12 * energies * slabs, order, 4 * first.size),
        name="map_product",
    )(first, second)


def convolve_body(count, energies, *refs):
    ins = refs[:count]
    outs = refs[count : count * (1 + energies)]
    green, screen, total = refs[count * (1 + energies) :]
    me = lax.axis_index("energy")
    points = count * energies
    middle = points // 2
    rows, columns = green.shape[2:]
    for k in range(count):
        base = (me ^ k) * energies
        for e in range(energies):
            green[:, base + e] = ins[k][0, :, e].astype(F32)
            screen[:, base + e] = ins[k][1, :, e].astype(F32)

    def tile(index, _):
        row = pl.multiple_of(index * 8, 8)
        for col in range(0, columns, 128):
            at = (pl.ds(row, 8), pl.ds(col, 128))
            gr = [green[(0, m) + at] for m in range(points)]
            gi = [green[(1, m) + at] for m in range(points)]
            wr = [screen[(0, m) + at] for m in range(points)]
            wi = [screen[(1, m) + at] for m in range(points)]
            for n in range(points):
                re = None
                im = None
                for m in range(points):
                    lag = n - m + middle
                    if 0 <= lag < points:
                        a = gr[m] * wr[lag] - gi[m] * wi[lag]
                        b = gr[m] * wi[lag] + gi[m] * wr[lag]
                        re = a if re is None else re + a
                        im = b if im is None else im + b
                total[(n, 0) + at] = -im / points
                total[(n, 1) + at] = re / points
        return 0

    lax.fori_loop(0, rows // 8, tile, 0)
    for k in range(count):
        base = (me ^ k) * energies
        for e in range(energies):
            outs[k * energies + e][...] = total[base + e].astype(BF16)


def convolve(pieces):
    count = len(pieces)
    _, _, energies, slabs, rows, columns = pieces[0].shape
    in_spec = pl.BlockSpec((2, 2, energies, None, rows, columns), lambda s: (0, 0, 0, s, 0, 0))
    out_spec = pl.BlockSpec((None, 2, rows, columns), lambda s: (s, 0, 0, 0))
    points = count * energies
    outs = pl.pallas_call(
        functools.partial(convolve_body, count, energies),
        grid=(slabs,),
        in_specs=[in_spec] * count,
        out_specs=[out_spec] * points,
        out_shape=[jax.ShapeDtypeStruct((slabs, 2, rows, columns), BF16)] * points,
        scratch_shapes=[
            pltpu.VMEM((2, points, rows, columns), F32),
            pltpu.VMEM((2, points, rows, columns), F32),
            pltpu.VMEM((points, 2, rows, columns), F32),
        ],
        compiler_params=params(),
        cost_estimate=pl.CostEstimate(
            flops=8 * 200 * slabs * rows * columns * points,
            bytes_accessed=6 * points * slabs * rows * columns * 2,
            transcendentals=0,
        ),
        name="convolve",
    )(*pieces)
    return [outs[k * energies : (k + 1) * energies] for k in range(count)]


def source_body(count, *refs):
    pieces = refs[:count]
    g_ref, k_ref, b_ref, v_ref, sigma, carry = refs[count:]
    me = lax.axis_index("energy")
    rows = pieces[0].shape[1]
    order = sigma.shape[1]
    for k in range(count):
        start = pl.multiple_of((me ^ k) * rows, rows)
        for part in range(2):
            sigma[part, pl.ds(start, rows), :] = pieces[k][part]
    left = jnp.concatenate([g_ref[0], g_ref[1]], axis=1)
    mixed = dot(left, panel(sigma[0], sigma[1])).astype(BF16)
    source = dot_nt(mixed, panel(g_ref[0], g_ref[1]))

    @pl.when(pl.program_id(0) == 0)
    def _():
        carry[...] = source

    @pl.when(pl.program_id(0) > 0)
    def _():
        high, low = panels(k_ref)
        inner = times_wide(high, low, carry[...])
        carry[...] = times_adjoint(inner, high, low) + source

    b_ref[...] = carry[...]

    @pl.when(pl.program_id(0) == pl.num_programs(0) - 1)
    def _():
        v_ref[...] = carry[...].astype(BF16)


def build_sources(pieces, green, kernels, energy):
    count = len(pieces)
    slabs, _, rows, order = pieces[0].shape
    piece_spec = pl.BlockSpec((None, 2, rows, order), lambda s: (s, 0, 0, 0))
    return pl.pallas_call(
        functools.partial(source_body, count),
        grid=(slabs,),
        in_specs=[piece_spec] * count
        + [
            pl.BlockSpec((2, None, None, order, order), lambda s: (0, energy, s, 0, 0)),
            pl.BlockSpec((None, None, 2, order, 2 * order), lambda s: (energy, s, 0, 0, 0)),
        ],
        out_specs=[
            pl.BlockSpec((None, order, 2 * order), lambda s: (s, 0, 0)),
            pl.BlockSpec((order, 2 * order), lambda s: (0, 0)),
        ],
        out_shape=[
            jax.ShapeDtypeStruct((slabs, order, 2 * order), F32),
            jax.ShapeDtypeStruct((order, 2 * order), BF16),
        ],
        scratch_shapes=[
            pltpu.VMEM((2, order, order), BF16),
            pltpu.VMEM((order, 2 * order), F32),
        ],
        compiler_params=params(),
        cost_estimate=cost(32 * slabs, order, 24 * slabs * order * order),
        name="sources",
    )(*pieces, green, kernels)


def combine_body(v_ref, t_ref, base_ref, *outs):
    order = v_ref.shape[0]
    high, low = panels(t_ref)
    inner = times_narrow(high, low, v_ref[:, :order], v_ref[:, order:])
    value = times_adjoint(inner, high, low) + base_ref[...].astype(F32)
    for out in outs:
        out[...] = value.astype(out.dtype)


def combine(arrived, maps, base, base_index, energy, dtypes):
    order = arrived.shape[0]
    whole = pl.BlockSpec((order, 2 * order), lambda i: (0, 0))
    if base_index is None:
        base_spec = whole
    else:
        base_spec = pl.BlockSpec((None, order, 2 * order), lambda i: (base_index, 0, 0))
    return pl.pallas_call(
        combine_body,
        grid=(1,),
        in_specs=[
            whole,
            pl.BlockSpec((None, 2, order, 2 * order), lambda i: (energy, 0, 0, 0)),
            base_spec,
        ],
        out_specs=[whole] * len(dtypes),
        out_shape=[jax.ShapeDtypeStruct((order, 2 * order), t) for t in dtypes],
        compiler_params=params(),
        cost_estimate=cost(20, order, 20 * order * order),
        name="combine",
    )(arrived, maps, base)


def entry_body(w_ref, p_ref, b_ref, y_ref):
    high, low = panels(p_ref)
    inner = times_wide(high, low, w_ref[...].astype(F32))
    y_ref[...] = times_adjoint(inner, high, low) + b_ref[...]


def apply_entry(entry, prefixes, sums, energy):
    slabs, order, _ = sums.shape
    block = pl.BlockSpec((None, order, 2 * order), lambda s: (s, 0, 0))
    return pl.pallas_call(
        entry_body,
        grid=(slabs,),
        in_specs=[
            pl.BlockSpec((order, 2 * order), lambda s: (0, 0)),
            pl.BlockSpec((None, None, 2, order, 2 * order), lambda s: (energy, s, 0, 0, 0)),
            block,
        ],
        out_specs=block,
        out_shape=jax.ShapeDtypeStruct(sums.shape, F32),
        compiler_params=params(),
        cost_estimate=cost(24 * slabs, order, 24 * slabs * order * order),
        name="entry",
    )(entry, prefixes, sums)


def finish_body(v_ref, r_ref, y_ref, *rest):
    out = rest[-1]
    order = v_ref.shape[0]
    high, low = panels(r_ref)
    inner = times_narrow(high, low, v_ref[:, :order], v_ref[:, order:])
    value = times_adjoint(inner, high, low) + y_ref[...]
    out[0] = value[:, :order]
    out[1] = value[:, order:]


def finish(arrived, maps, partial, energy, energies, held):
    slabs, order, _ = partial.shape
    operands = [arrived, maps, partial]
    in_specs = [
        pl.BlockSpec((order, 2 * order), lambda s: (0, 0)),
        pl.BlockSpec((None, None, 2, order, 2 * order), lambda s: (energy, s, 0, 0, 0)),
        pl.BlockSpec((None, order, 2 * order), lambda s: (s, 0, 0)),
    ]
    aliases = {}
    if held is not None:
        operands.append(held)
        in_specs.append(pl.BlockSpec(memory_space=pl.ANY))
        aliases = {3: 0}
    return pl.pallas_call(
        finish_body,
        grid=(slabs,),
        in_specs=in_specs,
        out_specs=pl.BlockSpec((2, None, None, order, order), lambda s: (0, energy, s, 0, 0)),
        out_shape=jax.ShapeDtypeStruct((2, energies, slabs, order, order), F32),
        input_output_aliases=aliases,
        compiler_params=params(),
        cost_estimate=cost(20 * slabs, order, 24 * slabs * order * order),
        name="finish",
    )(*operands)


def swap(x, k):
    count = lax.axis_size("energy")
    return lax.ppermute(x, "energy", [(i, i ^ k) for i in range(count)])


def forward(x, by):
    count = lax.axis_size("slab")
    return lax.ppermute(x, "slab", [(i, i + by) for i in range(count - by)])


CHUNKS = 2


def per_device(green_lesser, screened_lesser, green_retarded, coupling):
    count = lax.axis_size("energy")
    depth = lax.axis_size("slab")
    me = lax.axis_index("energy")
    _, energies, slabs, order, _ = green_lesser.shape
    rows = order // count
    partners = [k for k in range(count) if k >= 2] + [k for k in range(min(2, count)) if k == 1]

    def piece(k, start, size):
        sizes = (2, energies, size, rows, order)
        begin = (0, 0, start, (me ^ k) * rows, 0)
        return jnp.stack(
            [
                lax.dynamic_slice(green_lesser, begin, sizes),
                lax.dynamic_slice(screened_lesser, begin, sizes),
            ]
        )

    size = slabs // CHUNKS if slabs % CHUNKS == 0 else slabs
    rounds = [[None] * count for _ in range(slabs // size)]
    for index, held in enumerate(rounds):
        for k in partners:
            held[k] = swap(piece(k, index * size, size), k)
        held[0] = piece(0, index * size, size)

    kernels, prefixes = build_maps(green_retarded, coupling)
    steps = (depth - 1).bit_length()
    step_maps = [prefixes[:, slabs - 1]]
    gap_maps = [None]
    for k in range(steps - 1):
        arrived = forward(step_maps[k], 1 << k)
        if gap_maps[k] is None:
            gap_maps.append(arrived)
        else:
            gap_maps.append(map_product(gap_maps[k][:, None], arrived)[:, 0])
        if k < steps - 2:
            step_maps.append(map_product(step_maps[k][:, None], arrived)[:, 0])
    last_gap = gap_maps[-1] if steps > 0 else None
    final_maps = prefixes if last_gap is None else map_product(prefixes, last_gap)

    sigmas = [convolve(held) for held in rounds]

    result = None
    for e in range(energies):
        pieces = [None] * count
        for k in partners + [0]:
            block = jnp.concatenate([chunk[k][e] for chunk in sigmas], axis=0)
            pieces[k] = block if k == 0 else swap(block, k)
        sums, carry = build_sources(pieces, green_retarded, kernels, e)
        running, index = sums, slabs - 1
        entry = None
        for k in range(steps):
            arrived = forward(carry, 1 << k)
            if k == steps - 1:
                break
            if k == steps - 2:
                (carry,) = combine(arrived, step_maps[k], running, index, e, (BF16,))
            else:
                running, carry = combine(arrived, step_maps[k], running, index, e, (F32, BF16))
                index = None
            if entry is None:
                entry = arrived
            else:
                (entry,) = combine(arrived, gap_maps[k], entry, None, e, (F32,))
        partial = sums if entry is None else apply_entry(entry, prefixes, sums, e)
        result = finish(arrived, final_maps, partial, e, energies, result)
    return result


def solution(mesh):
    placed = (
        P(None, "energy", "slab", None, None),
        P(None, "energy", "slab", None, None),
        P(None, "energy", "slab", None, None),
        P(None, "slab", None, None),
    )
    return jax.shard_map(
        per_device,
        mesh=mesh,
        in_specs=placed,
        out_specs=P(None, "energy", "slab", None, None),
        check_vma=False,
    )
```

```python
import functools

import jax
import jax.numpy as jnp
from jax import lax
from jax.experimental import pallas as pl
from jax.experimental.pallas import tpu as pltpu
from jax.sharding import PartitionSpec as P

BF16 = jnp.bfloat16
F32 = jnp.float32
VMEM_LIMIT = 24 * 1024 * 1024


def params():
    return pltpu.CompilerParams(vmem_limit_bytes=VMEM_LIMIT)


def ordered(body, count, extra=1):
    def run(*refs):
        body(*refs[:count], *refs[count + extra :])

    return run


ANYWHERE = pl.BlockSpec(memory_space=pl.ANY)


def cost():
    return pl.CostEstimate(flops=0, bytes_accessed=0, transcendentals=0)


def split(value):
    high = value.astype(BF16)
    low = (value - high.astype(F32)).astype(BF16)
    return high, low


def panel(re, im):
    return jnp.concatenate(
        [jnp.concatenate([re, im], axis=1), jnp.concatenate([-im, re], axis=1)], axis=0
    )


def dot(left, right):
    return lax.dot_general(left, right, (((1,), (0,)), ((), ())), preferred_element_type=F32)


def dot_nt(left, right):
    return lax.dot_general(left, right, (((1,), (1,)), ((), ())), preferred_element_type=F32)


def times_wide(a_high, a_low, x):
    order = x.shape[0]
    x_high, x_low = split(x)
    xh = panel(x_high[:, :order], x_high[:, order:])
    xl = panel(x_low[:, :order], x_low[:, order:])
    left = jnp.concatenate([a_high, a_high, a_low], axis=1)
    return dot(left, jnp.concatenate([xh, xl, xh], axis=0))


def times_narrow(a_high, a_low, re, im):
    xp = panel(re, im)
    left = jnp.concatenate([a_high, a_low], axis=1)
    return dot(left, jnp.concatenate([xp, xp], axis=0))


def times_adjoint(y, t_high, t_low):
    order = y.shape[0]
    y_high, y_low = split(y)
    th = panel(t_high[:, :order], t_high[:, order:])
    tl = panel(t_low[:, :order], t_low[:, order:])
    left = jnp.concatenate([y_high, y_low, y_high], axis=1)
    return dot_nt(left, jnp.concatenate([th, th, tl], axis=1))


def panels(ref):
    return ref[0], ref[1]


def store_map(ref, value):
    high, low = split(value)
    ref[0] = high
    ref[1] = low


def pack_body(wanted, *refs):
    sources, outs, sems = refs[:2], refs[-1 - len(wanted) : -1], refs[-1]
    copies = []
    for out, (k, start) in zip(outs, wanted):
        size, rows = out.shape[3:5]
        begin = pl.multiple_of((lax.axis_index("energy") ^ k) * rows, rows)
        for part in range(2):
            block = sources[part].at[:, :, pl.ds(start, size), pl.ds(begin, rows), :]
            copies.append(pltpu.make_async_copy(block, out.at[part], sems.at[len(copies)]))
    for copy in copies:
        copy.start()
    for copy in copies:
        copy.wait()


def pack(green, screen, wanted, count, *after):
    _, energies, _, order, _ = green.shape
    shapes = [(2, 2, energies, size, order // count, order) for _, _, size in wanted]
    return pl.pallas_call(
        functools.partial(pack_body, [w[:2] for w in wanted]),
        in_specs=[ANYWHERE] * (2 + len(after)),
        out_specs=[pl.BlockSpec(memory_space=pltpu.VMEM)] * len(wanted),
        out_shape=[jax.ShapeDtypeStruct(shape, BF16) for shape in shapes],
        scratch_shapes=[pltpu.SemaphoreType.DMA((2 * len(wanted),))],
        compiler_params=params(),
        cost_estimate=cost(),
        name="pack",
    )(green, screen, *after)


def maps_body(g_ref, c_ref, k_ref, p_ref, carry):
    left = jnp.concatenate([g_ref[0], g_ref[1]], axis=1)
    value = dot(left, panel(c_ref[0], c_ref[1]))
    store_map(k_ref, value)

    @pl.when(pl.program_id(1) == 0)
    def _():
        carry[...] = value

    @pl.when(pl.program_id(1) > 0)
    def _():
        high, low = panels(k_ref)
        carry[...] = times_wide(high, low, carry[...])

    store_map(p_ref, carry[...])


def build_maps(green, coupling, *after):
    _, energies, slabs, order, _ = green.shape
    shape = jax.ShapeDtypeStruct((energies, slabs, 2, order, 2 * order), BF16)
    out_spec = pl.BlockSpec((None, None, 2, order, 2 * order), lambda e, s: (e, s, 0, 0, 0))
    return pl.pallas_call(
        lambda *refs: maps_body(*refs[:2], *refs[2 + len(after) :]),
        grid=(energies, slabs),
        in_specs=[
            pl.BlockSpec((2, None, None, order, order), lambda e, s: (0, e, s, 0, 0)),
            pl.BlockSpec((2, None, order, order), lambda e, s: (0, s, 0, 0)),
        ]
        + [ANYWHERE] * len(after),
        out_specs=[out_spec, out_spec],
        out_shape=[shape, shape],
        scratch_shapes=[pltpu.VMEM((order, 2 * order), F32)],
        compiler_params=params(),
        cost_estimate=cost(),
        name="maps",
    )(green, coupling, *after)


def one_map(maps, energy):
    if isinstance(maps, list):
        return maps[energy], pl.BlockSpec(maps[energy].shape, lambda *_: (0, 0, 0))
    return maps, pl.BlockSpec((None,) + maps.shape[1:], lambda *_: (energy, 0, 0, 0))


def map_product_body(energies, *refs):
    out = refs[-1]
    for e in range(energies):
        high, low = panels(refs[2 * e])
        other = refs[2 * e + 1]
        store_map(out.at[e], times_wide(high, low, other[0].astype(F32) + other[1].astype(F32)))


def map_product(first, second, energies, after):
    pairs = [one_map(maps, e) for e in range(energies) for maps in (first, second)]
    shape = (energies,) + pairs[0][1].block_shape[-3:]
    return pl.pallas_call(
        ordered(functools.partial(map_product_body, energies), 2 * energies),
        grid=(1,),
        in_specs=[spec for _, spec in pairs] + [ANYWHERE],
        out_specs=pl.BlockSpec(shape, lambda i: (0, 0, 0, 0)),
        out_shape=jax.ShapeDtypeStruct(shape, BF16),
        compiler_params=params(),
        cost_estimate=cost(),
        name="map_product",
    )(*[maps for maps, _ in pairs], after)


def pair_maps_body(energies, *refs):
    step, plane, inner = refs[-3:]
    odd = (lax.axis_index("slab") & 1) == 1
    for e in range(energies):
        mine, other = refs[2 * e], refs[2 * e + 1]
        order = mine.shape[1]
        first = [jnp.where(odd, mine[part], other[part]) for part in range(2)]
        second = [jnp.where(odd, other[part], mine[part]).astype(F32) for part in range(2)]
        store_map(plane.at[e], times_wide(*first, second[0] + second[1]))
        row = lax.broadcasted_iota(jnp.int32, (order, 2 * order), 0)
        column = lax.broadcasted_iota(jnp.int32, (order, 2 * order), 1)
        unit = jnp.where(row == column, 1.0, 0.0)
        for part in range(2):
            step[e, part] = first[part]
            identity = unit if part == 0 else jnp.zeros_like(unit)
            inner[e, part] = jnp.where(odd, other[part].astype(F32), identity).astype(BF16)


def pair_maps(mine, other, energies, after):
    pairs = [one_map(maps, e) for e in range(energies) for maps in (mine, other)]
    shape = (energies,) + pairs[0][1].block_shape[-3:]
    return pl.pallas_call(
        ordered(functools.partial(pair_maps_body, energies), 2 * energies),
        grid=(1,),
        in_specs=[spec for _, spec in pairs] + [ANYWHERE],
        out_specs=[pl.BlockSpec(shape, lambda i: (0, 0, 0, 0))] * 3,
        out_shape=[jax.ShapeDtypeStruct(shape, BF16)] * 3,
        compiler_params=params(),
        cost_estimate=cost(),
        name="pair_maps",
    )(*[maps for maps, _ in pairs], after)


def convolve_body(count, energies, shared, *refs):
    ins, outs = refs[:count], refs[count + 1 + shared :]
    green, screen, total = refs[-3:]
    me = lax.axis_index("energy")
    points = count * energies
    middle = points // 2
    rows, columns = green.shape[2:]
    for k in range(count):
        base = (me ^ k) * energies
        for e in range(energies):
            green[:, base + e] = ins[k][0, :, e].astype(F32)
            screen[:, base + e] = ins[k][1, :, e].astype(F32)

    def tile(index, _):
        row = pl.multiple_of(index * 8, 8)
        for col in range(0, columns, 128):
            at = (pl.ds(row, 8), pl.ds(col, 128))
            gr = [green[(0, m) + at] for m in range(points)]
            gi = [green[(1, m) + at] for m in range(points)]
            wr = [screen[(0, m) + at] for m in range(points)]
            wi = [screen[(1, m) + at] for m in range(points)]
            for n in range(points):
                re = None
                im = None
                for m in range(points):
                    lag = n - m + middle
                    if 0 <= lag < points:
                        a = gr[m] * wr[lag] - gi[m] * wi[lag]
                        b = gr[m] * wi[lag] + gi[m] * wr[lag]
                        re = a if re is None else re + a
                        im = b if im is None else im + b
                total[(n, 0) + at] = -im / points
                total[(n, 1) + at] = re / points
        return 0

    lax.fori_loop(0, rows // 8, tile, 0)
    for k in range(count):
        base = (me ^ k) * energies
        for e in range(energies):
            outs[k * energies + e][...] = total[base + e].astype(BF16)


def convolve(pieces, near, start, slabs, size, held, after):
    count = len(pieces)
    _, _, energies, _, rows, columns = pieces[0].shape
    block = (2, 2, energies, None, rows, columns)
    points = count * energies
    part = pl.BlockSpec((None, 2, rows, columns), lambda s: (s, 0, 0, 0))
    whole = pl.BlockSpec((None, 2, rows, columns), lambda s: (s + start, 0, 0, 0))
    later = [index for index in range(points) if index % energies or index // energies in near]
    outs = pl.pallas_call(
        functools.partial(convolve_body, count, energies, len(held)),
        grid=(size,),
        in_specs=[
            pl.BlockSpec(block, lambda s, first=start if x.shape[3] == slabs else 0: (0, 0, 0, s + first, 0, 0))
            for x in pieces
        ]
        + [ANYWHERE] * (1 + len(held)),
        out_specs=[whole if index in later else part for index in range(points)],
        out_shape=[
            jax.ShapeDtypeStruct((slabs if index in later else size, 2, rows, columns), BF16)
            for index in range(points)
        ],
        input_output_aliases={count + 1 + i: later[i] for i in range(len(held))},
        scratch_shapes=[
            pltpu.VMEM((2, points, rows, columns), F32),
            pltpu.VMEM((2, points, rows, columns), F32),
            pltpu.VMEM((points, 2, rows, columns), F32),
        ],
        compiler_params=params(),
        cost_estimate=cost(),
        name="convolve",
    )(*pieces, after, *held)
    return [outs[k * energies : (k + 1) * energies] for k in range(count)], [outs[index] for index in later]


def source_body(owners, *refs):
    pieces = refs[: len(owners)]
    g_ref, k_ref, b_ref, v_ref, sigma, carry = refs[len(owners) :]
    me = lax.axis_index("energy")
    step = pl.program_id(0)
    for piece, (k, first) in zip(pieces, owners):
        size, _, rows, _ = piece.shape

        def place(piece=piece, k=k, first=first, rows=rows):
            start = pl.multiple_of((me ^ k) * rows, rows)
            for part in range(2):
                sigma[part, pl.ds(start, rows), :] = piece[step - first, part]

        pl.when((step >= first) & (step < first + size))(place)

    left = jnp.concatenate([g_ref[0], g_ref[1]], axis=1)
    mixed = dot(left, panel(sigma[0], sigma[1])).astype(BF16)
    source = dot_nt(mixed, panel(g_ref[0], g_ref[1]))

    @pl.when(step == 0)
    def _():
        carry[...] = source

    @pl.when(step > 0)
    def _():
        high, low = panels(k_ref)
        inner = times_wide(high, low, carry[...])
        carry[...] = times_adjoint(inner, high, low) + source

    b_ref[...] = carry[...]

    @pl.when(step == pl.num_programs(0) - 1)
    def _():
        v_ref[...] = carry[...].astype(BF16)


def build_sources(pieces, green, kernels, energy, after):
    slabs, order = green.shape[2:4]
    flat = [piece for group in pieces for piece in group]
    owners = []
    for k, group in enumerate(pieces):
        first = 0
        for piece in group:
            owners.append((k, first))
            first += piece.shape[0]
    return pl.pallas_call(
        ordered(functools.partial(source_body, owners), len(flat) + 2),
        grid=(slabs,),
        in_specs=[pl.BlockSpec(x.shape, lambda s: (0, 0, 0, 0)) for x in flat]
        + [
            pl.BlockSpec((2, None, None, order, order), lambda s: (0, energy, s, 0, 0)),
            pl.BlockSpec((None, None, 2, order, 2 * order), lambda s: (energy, s, 0, 0, 0)),
            ANYWHERE,
        ],
        out_specs=[
            pl.BlockSpec((None, order, 2 * order), lambda s: (s, 0, 0)),
            pl.BlockSpec((order, 2 * order), lambda s: (0, 0)),
        ],
        out_shape=[
            jax.ShapeDtypeStruct((slabs, order, 2 * order), F32),
            jax.ShapeDtypeStruct((order, 2 * order), BF16),
        ],
        scratch_shapes=[
            pltpu.VMEM((2, order, order), BF16),
            pltpu.VMEM((order, 2 * order), F32),
        ],
        compiler_params=params(),
        cost_estimate=cost(),
        name="sources",
    )(*flat, green, kernels, after)


def congruence(t_ref, x):
    order = x.shape[0]
    high, low = panels(t_ref)
    if x.dtype == F32:
        inner = times_wide(high, low, x)
    else:
        inner = times_narrow(high, low, x[:, :order], x[:, order:])
    return times_adjoint(inner, high, low)


def total(refs):
    value = refs[0][...]
    for ref in refs[1:]:
        value = value + ref[...]
    return value


def pair_body(v_ref, own_ref, sum_ref, t_ref, full_ref, short_ref):
    odd = (lax.axis_index("slab") & 1) == 1
    x = jnp.where(odd, v_ref[...], own_ref[...])
    base = jnp.where(odd, sum_ref[...], v_ref[...].astype(F32))
    value = base + congruence(t_ref, x)
    full_ref[...] = value
    short_ref[...] = value.astype(BF16)


def pair_sum(arrived, own, sums, maps, energy, *after):
    slabs, order, _ = sums.shape
    step, step_spec = one_map(maps, energy)
    whole = pl.BlockSpec((order, 2 * order), lambda i: (0, 0))
    return pl.pallas_call(
        ordered(pair_body, 4, len(after)),
        grid=(1,),
        in_specs=[whole, whole, pl.BlockSpec((None, order, 2 * order), lambda i: (slabs - 1, 0, 0)), step_spec]
        + [ANYWHERE] * len(after),
        out_specs=[whole] * 2,
        out_shape=[jax.ShapeDtypeStruct((order, 2 * order), t) for t in (F32, BF16)],
        compiler_params=params(),
        cost_estimate=cost(),
        name="pair_sum",
    )(arrived, own, sums, step, *after)


def combine_body(arrivals, t_ref, base_ref, outs):
    value = congruence(t_ref, total(arrivals)) + base_ref[...].astype(F32)
    for out in outs:
        out[...] = value.astype(out.dtype)


def combine(arrived, maps, base, energy, dtypes, *after):
    order = arrived[0].shape[0]
    if isinstance(base, list):
        base = functools.reduce(jnp.add, base)
    step, step_spec = one_map(maps, energy)
    whole = pl.BlockSpec((order, 2 * order), lambda i: (0, 0))
    count = len(arrived)

    def body(*refs):
        combine_body(refs[:count], refs[count], refs[count + 1], refs[count + 2 + len(after) :])

    return pl.pallas_call(
        body,
        grid=(1,),
        in_specs=[whole] * count + [step_spec, whole] + [ANYWHERE] * len(after),
        out_specs=[whole] * len(dtypes),
        out_shape=[jax.ShapeDtypeStruct((order, 2 * order), t) for t in dtypes],
        compiler_params=params(),
        cost_estimate=cost(),
        name="combine",
    )(*arrived, step, base, *after)


def entry_body(arrivals, t_ref, base_ref, out):
    odd = (lax.axis_index("slab") & 1) == 1
    base = jnp.where(odd, base_ref[...].astype(F32), 0.0)
    out[...] = base + congruence(t_ref, total(arrivals))


def pair_entry(arrived, maps, before, energy, *after):
    order = arrived[0].shape[0]
    step, step_spec = one_map(maps, energy)
    whole = pl.BlockSpec((order, 2 * order), lambda i: (0, 0))
    count = len(arrived)

    def body(*refs):
        entry_body(refs[:count], refs[count], refs[count + 1], refs[-1])

    return pl.pallas_call(
        body,
        grid=(1,),
        in_specs=[whole] * count + [step_spec, whole] + [ANYWHERE] * len(after),
        out_specs=whole,
        out_shape=jax.ShapeDtypeStruct((order, 2 * order), F32),
        compiler_params=params(),
        cost_estimate=cost(),
        name="pair_entry",
    )(*arrived, step, before, *after)


def finish_body(arrivals, q_ref, w_ref, p_ref, b_ref, *rest):
    out, entry = rest[-2:]
    order = entry.shape[0]

    @pl.when(pl.program_id(0) == 0)
    def _():
        value = total(arrivals)
        if q_ref is None:
            entry[...] = value.astype(F32)
        else:
            entry[...] = congruence(q_ref, value) + w_ref[...].astype(F32)

    high, low = panels(p_ref)
    inner = times_wide(high, low, entry[...])
    value = times_adjoint(inner, high, low) + b_ref[...]
    out[0] = value[:, :order]
    out[1] = value[:, order:]


def finish(arrived, gap, entry, prefixes, sums, energy, held, after):
    energies, slabs, _, order, _ = prefixes.shape
    whole = pl.BlockSpec((order, 2 * order), lambda s: (0, 0))
    operands = list(arrived)
    in_specs = [whole] * len(arrived)
    if gap is not None:
        step, step_spec = one_map(gap, energy)
        operands += [step, entry]
        in_specs += [step_spec, whole]
    operands += [prefixes, sums, after]
    in_specs += [
        pl.BlockSpec((None, None, 2, order, 2 * order), lambda s: (energy, s, 0, 0, 0)),
        pl.BlockSpec((None, order, 2 * order), lambda s: (s, 0, 0)),
        ANYWHERE,
    ]
    aliases = {}
    if held is not None:
        aliases = {len(operands): 0}
        operands.append(held)
        in_specs.append(ANYWHERE)

    def body(*refs):
        arrivals, rest = refs[: len(arrived)], refs[len(arrived) :]
        finish_body(arrivals, *((None, None) if gap is None else ()), *rest)

    return pl.pallas_call(
        body,
        grid=(slabs,),
        in_specs=in_specs,
        out_specs=pl.BlockSpec((2, None, None, order, order), lambda s: (0, energy, s, 0, 0)),
        out_shape=jax.ShapeDtypeStruct((2, energies, slabs, order, order), F32),
        input_output_aliases=aliases,
        scratch_shapes=[pltpu.VMEM((order, 2 * order), F32)],
        compiler_params=params(),
        cost_estimate=cost(),
        name="finish",
    )(*operands)


def swap(x, k):
    count = lax.axis_size("energy")
    return lax.ppermute(x, "energy", [(i, i ^ k) for i in range(count)])


def other_of_pair(x):
    return lax.ppermute(x, "slab", [(i, i ^ 1) for i in range(lax.axis_size("slab"))])


def forward(x, by, chosen):
    count = lax.axis_size("slab")
    return lax.ppermute(x, "slab", [(i, i + 2 * by) for i in range(count - 2 * by) if chosen(i // 2)])


def cut(slabs):
    return [(0, slabs - 1), (slabs - 1, 1)] if slabs > 1 else [(0, slabs)]


def per_device(green_lesser, screened_lesser, green_retarded, coupling):
    count = lax.axis_size("energy")
    depth = lax.axis_size("slab")
    if depth % 2 or count & (count - 1):
        raise ValueError("mesh axes")
    _, energies, slabs, order, _ = green_lesser.shape
    far = [k for k in range(count) if k >= 2]
    near = [k for k in range(min(2, count))]
    parts = cut(slabs)

    def first_rows(k, size):
        rows = order // count
        begin = (0, 0, 0, (lax.axis_index("energy") ^ k) * rows, 0)
        sizes = (2, energies, size, rows, order)
        return jnp.stack([lax.dynamic_slice(x, begin, sizes) for x in (green_lesser, screened_lesser)])

    pieces = [[None] * count for _ in parts]
    for k in near[1:]:
        for group in pieces:
            group[k] = swap(first_rows(k, slabs), k) if group is pieces[0] else pieces[0][k]
    for k in far:
        pieces[0][k] = swap(first_rows(k, parts[0][1]), k)
    tokens = [pieces[0][k] for k in near[1:]]
    places = [(chunk, k) for chunk in range(1, len(parts)) for k in far]
    wanted = [(k,) + parts[chunk] for chunk, k in places] + [(0, 0, slabs)]
    packed = pack(green_lesser, screened_lesser, wanted, count, *tokens)
    for (chunk, k), block in zip(places, packed):
        pieces[chunk][k] = swap(block, k)
    for group in pieces:
        group[0] = packed[-1]

    kernels, prefixes = build_maps(green_retarded, coupling, packed[-1])
    token = kernels
    mine = [prefixes[e, slabs - 1] for e in range(energies)]
    other = [other_of_pair(x) for x in mine]

    sigma = [[[] for _ in range(count)] for _ in range(energies)]
    held = []
    for chunk, (start, size) in enumerate(parts):
        if chunk == len(parts) - 1:
            pair_step, plane, inner = pair_maps(mine, other, energies, token)
            token = plane
        blocks, held = convolve(pieces[chunk], near, start, slabs, size, held, token)
        token = blocks[0][0]
        for k in far:
            sigma[0][k].append(swap(blocks[k][0], k))
    for e in range(energies):
        for k in near + far:
            if e > 0 or k in near:
                sigma[e][k].append(swap(blocks[k][e], k) if k else blocks[k][e])

    steps = (depth // 2 - 1).bit_length()
    step_maps, gap_maps = [plane], [None]

    def extend(k, token):
        least = 1 << k if k == steps - 2 else 0
        arrived = forward(step_maps[k], 1 << k, lambda pair: pair >= least)
        if k < steps - 2:
            token = map_product(step_maps[k], arrived, energies, token)
            step_maps.append(token)
        if gap_maps[k] is None:
            gap_maps.append(arrived)
        else:
            token = map_product(gap_maps[k], arrived, energies, token)
            gap_maps.append(token)
        return token

    for k in range(steps - 2):
        token = extend(k, token)
    nothing = jnp.zeros((order, 2 * order), BF16)
    sums, own, before = [None] * energies, [None] * energies, [None] * energies
    running, carry = [None] * energies, [None] * energies
    entry, arrived = [[nothing]] * energies, [None] * energies
    final = [[] for _ in range(energies)]

    def send(e, k):
        if k < steps - 1:
            arrived[e] = [
                forward(carry[e], 1 << k, lambda pair, bit=bit: (pair >> k) & 1 == bit) for bit in range(2)
            ]
        if steps > 0:
            final[e].append(forward(carry[e], 1 << (steps - 1), lambda pair: pair.bit_length() == k))

    for e in range(energies):
        sums[e], own[e] = build_sources(sigma[e], green_retarded, kernels, e, token)
        token = own[e]
        before[e] = other_of_pair(own[e])
    for e in range(energies):
        running[e], carry[e] = pair_sum(before[e], own[e], sums[e], pair_step, e, token)
        token = carry[e]
        send(e, 0)
    gap = inner
    for k in range(steps - 1):
        if k == steps - 2:
            token = extend(k, token)
            gap = token = map_product(inner, gap_maps[-1], energies, token)
        for e in range(energies):
            last = k == steps - 2
            made = combine(
                arrived[e][:1] if last else arrived[e],
                step_maps[k],
                running[e],
                e,
                (BF16,) if last else (F32, BF16),
                token,
                final[e][k],
            )
            token = carry[e] = made[-1]
            got, running[e] = arrived[e], made[0]
            send(e, k + 1)
            if k == 0:
                entry[e] = got
            else:
                entry[e] = list(combine(got, gap_maps[k], entry[e], e, (F32,), token))
                token = entry[e][0]
    for e in range(energies):
        entry[e] = token = pair_entry(entry[e], inner, before[e], e, token)
    result = None
    for e in range(energies):
        result = finish(final[e] or [nothing], gap, entry[e], prefixes, sums[e], e, result, token)
    return result


def solution(mesh):
    placed = (
        P(None, "energy", "slab", None, None),
        P(None, "energy", "slab", None, None),
        P(None, "energy", "slab", None, None),
        P(None, "slab", None, None),
    )
    return jax.shard_map(
        per_device,
        mesh=mesh,
        in_specs=placed,
        out_specs=P(None, "energy", "slab", None, None),
        check_vma=False,
    )
```

```python
import functools

import jax
import jax.numpy as jnp
from jax import lax
from jax.experimental import pallas as pl
from jax.experimental.pallas import tpu as pltpu
from jax.sharding import PartitionSpec as P

BF16 = jnp.bfloat16
F32 = jnp.float32
VMEM_LIMIT = 24 * 1024 * 1024


def params():
    return pltpu.CompilerParams(vmem_limit_bytes=VMEM_LIMIT)


def ordered(body, count, extra=1):
    def run(*refs):
        body(*refs[:count], *refs[count + extra :])

    return run


ANYWHERE = pl.BlockSpec(memory_space=pl.ANY)


def cost():
    return pl.CostEstimate(flops=0, bytes_accessed=0, transcendentals=0)


def split(value):
    high = value.astype(BF16)
    low = (value - high.astype(F32)).astype(BF16)
    return high, low


def panel(re, im):
    return jnp.concatenate(
        [jnp.concatenate([re, im], axis=1), jnp.concatenate([-im, re], axis=1)], axis=0
    )


def dot(left, right):
    return lax.dot_general(left, right, (((1,), (0,)), ((), ())), preferred_element_type=F32)


def dot_nt(left, right):
    return lax.dot_general(left, right, (((1,), (1,)), ((), ())), preferred_element_type=F32)


def times_wide(a_high, a_low, x):
    order = x.shape[0]
    x_high, x_low = split(x)
    xh = panel(x_high[:, :order], x_high[:, order:])
    xl = panel(x_low[:, :order], x_low[:, order:])
    left = jnp.concatenate([a_high, a_high, a_low], axis=1)
    return dot(left, jnp.concatenate([xh, xl, xh], axis=0))


def times_narrow(a_high, a_low, re, im):
    xp = panel(re, im)
    left = jnp.concatenate([a_high, a_low], axis=1)
    return dot(left, jnp.concatenate([xp, xp], axis=0))


def times_adjoint(y, t_high, t_low):
    order = y.shape[0]
    y_high, y_low = split(y)
    th = panel(t_high[:, :order], t_high[:, order:])
    tl = panel(t_low[:, :order], t_low[:, order:])
    left = jnp.concatenate([y_high, y_low, y_high], axis=1)
    return dot_nt(left, jnp.concatenate([th, th, tl], axis=1))


def panels(ref):
    return ref[0], ref[1]


def store_map(ref, value):
    high, low = split(value)
    ref[0] = high
    ref[1] = low


def pack_body(wanted, *refs):
    sources, outs, sems = refs[:2], refs[-1 - len(wanted) : -1], refs[-1]
    copies = []
    for out, (parts, k, start) in zip(outs, wanted):
        size, rows = out.shape[-4 + 1 : -1]
        begin = pl.multiple_of((lax.axis_index("energy") ^ k) * rows, rows)
        for part in parts:
            block = sources[part].at[:, :, pl.ds(start, size), pl.ds(begin, rows), :]
            target = out if len(parts) == 1 else out.at[part]
            copies.append(pltpu.make_async_copy(block, target, sems.at[len(copies)]))
    for copy in copies:
        copy.start()
    for copy in copies:
        copy.wait()


def pack(green, screen, wanted, count, *after):
    _, energies, _, order, _ = green.shape
    shapes = [
        (len(parts),) * (len(parts) > 1) + (2, energies, size, order // count, order)
        for parts, _, _, size in wanted
    ]
    return pl.pallas_call(
        functools.partial(pack_body, [w[:3] for w in wanted]),
        in_specs=[ANYWHERE] * (2 + len(after)),
        out_specs=[pl.BlockSpec(memory_space=pltpu.VMEM)] * len(wanted),
        out_shape=[jax.ShapeDtypeStruct(shape, BF16) for shape in shapes],
        scratch_shapes=[pltpu.SemaphoreType.DMA((sum(len(w[0]) for w in wanted),))],
        compiler_params=params(),
        cost_estimate=cost(),
        name="pack",
    )(green, screen, *after)


def maps_body(g_ref, c_ref, k_ref, p_ref, carry):
    left = jnp.concatenate([g_ref[0], g_ref[1]], axis=1)
    value = dot(left, panel(c_ref[0], c_ref[1]))
    store_map(k_ref, value)

    @pl.when(pl.program_id(1) == 0)
    def _():
        carry[...] = value

    @pl.when(pl.program_id(1) > 0)
    def _():
        high, low = panels(k_ref)
        carry[...] = times_wide(high, low, carry[...])

    store_map(p_ref, carry[...])


def build_maps(green, coupling, *after):
    _, energies, slabs, order, _ = green.shape
    shape = jax.ShapeDtypeStruct((energies, slabs, 2, order, 2 * order), BF16)
    out_spec = pl.BlockSpec((None, None, 2, order, 2 * order), lambda e, s: (e, s, 0, 0, 0))
    return pl.pallas_call(
        lambda *refs: maps_body(*refs[:2], *refs[2 + len(after) :]),
        grid=(energies, slabs),
        in_specs=[
            pl.BlockSpec((2, None, None, order, order), lambda e, s: (0, e, s, 0, 0)),
            pl.BlockSpec((2, None, order, order), lambda e, s: (0, s, 0, 0)),
        ]
        + [ANYWHERE] * len(after),
        out_specs=[out_spec, out_spec],
        out_shape=[shape, shape],
        scratch_shapes=[pltpu.VMEM((order, 2 * order), F32)],
        compiler_params=params(),
        cost_estimate=cost(),
        name="maps",
    )(green, coupling, *after)


def one_map(maps, energy):
    if isinstance(maps, list):
        return maps[energy], pl.BlockSpec(maps[energy].shape, lambda *_: (0, 0, 0))
    return maps, pl.BlockSpec((None,) + maps.shape[1:], lambda *_: (energy, 0, 0, 0))


def pair_maps_body(energies, *refs):
    step, plane, inner = refs[-3:]
    odd = (lax.axis_index("slab") & 1) == 1
    for e in range(energies):
        mine, other = refs[2 * e], refs[2 * e + 1]
        order = mine.shape[1]
        first = [jnp.where(odd, mine[part], other[part]) for part in range(2)]
        second = [jnp.where(odd, other[part], mine[part]).astype(F32) for part in range(2)]
        store_map(plane.at[e], times_wide(*first, second[0] + second[1]))
        row = lax.broadcasted_iota(jnp.int32, (order, 2 * order), 0)
        column = lax.broadcasted_iota(jnp.int32, (order, 2 * order), 1)
        unit = jnp.where(row == column, 1.0, 0.0)
        for part in range(2):
            step[e, part] = first[part]
            identity = unit if part == 0 else jnp.zeros_like(unit)
            inner[e, part] = jnp.where(odd, other[part].astype(F32), identity).astype(BF16)


def pair_maps(mine, other, energies, after):
    pairs = [one_map(maps, e) for e in range(energies) for maps in (mine, other)]
    shape = (energies,) + pairs[0][1].block_shape[-3:]
    return pl.pallas_call(
        ordered(functools.partial(pair_maps_body, energies), 2 * energies),
        grid=(1,),
        in_specs=[spec for _, spec in pairs] + [ANYWHERE],
        out_specs=[pl.BlockSpec(shape, lambda i: (0, 0, 0, 0))] * 3,
        out_shape=[jax.ShapeDtypeStruct(shape, BF16)] * 3,
        compiler_params=params(),
        cost_estimate=cost(),
        name="pair_maps",
    )(*[maps for maps, _ in pairs], after)


def convolve_body(pairs, energies, shared, *refs):
    count = len(pairs)
    taken = sum(1 + pair for pair in pairs)
    ins, outs = list(refs[:taken]), refs[taken + 1 + shared :]
    green, screen, total = refs[-3:]
    me = lax.axis_index("energy")
    points = count * energies
    middle = points // 2
    rows, columns = green.shape[2:]
    for k in range(count):
        base = (me ^ k) * energies
        piece = ins.pop(0)
        halves = (piece, ins.pop(0)) if pairs[k] else (piece.at[0], piece.at[1])
        for e in range(energies):
            green[:, base + e] = halves[0][:, e].astype(F32)
            screen[:, base + e] = halves[1][:, e].astype(F32)

    def tile(index, _):
        row = pl.multiple_of(index * 8, 8)
        for col in range(0, columns, 128):
            at = (pl.ds(row, 8), pl.ds(col, 128))
            gr = [green[(0, m) + at] for m in range(points)]
            gi = [green[(1, m) + at] for m in range(points)]
            wr = [screen[(0, m) + at] for m in range(points)]
            wi = [screen[(1, m) + at] for m in range(points)]
            for n in range(points):
                re = None
                im = None
                for m in range(points):
                    lag = n - m + middle
                    if 0 <= lag < points:
                        a = gr[m] * wr[lag] - gi[m] * wi[lag]
                        b = gr[m] * wi[lag] + gi[m] * wr[lag]
                        re = a if re is None else re + a
                        im = b if im is None else im + b
                total[(n, 0) + at] = -im / points
                total[(n, 1) + at] = re / points
        return 0

    lax.fori_loop(0, rows // 8, tile, 0)
    for k in range(count):
        base = (me ^ k) * energies
        for e in range(energies):
            outs[k * energies + e][...] = total[base + e].astype(BF16)


def convolve(pieces, start, slabs, size, held, after):
    count = len(pieces)
    pairs = [isinstance(piece, tuple) for piece in pieces]
    operands, in_specs = [], []
    for piece, pair in zip(pieces, pairs):
        if pair:
            operands += piece
            energies, _, rows, columns = piece[0].shape[1:]
            in_specs += [pl.BlockSpec((2, energies, None, rows, columns), lambda s: (0, 0, s + start, 0, 0))] * 2
        else:
            operands.append(piece)
            energies, _, rows, columns = piece.shape[2:]
            first = start if piece.shape[3] == slabs else 0
            block = (2, 2, energies, None, rows, columns)
            in_specs.append(pl.BlockSpec(block, lambda s, first=first: (0, 0, 0, s + first, 0, 0)))
    points = count * energies
    whole = pl.BlockSpec((None, 2, rows, columns), lambda s: (s + start, 0, 0, 0))
    outs = pl.pallas_call(
        functools.partial(convolve_body, pairs, energies, len(held)),
        grid=(size,),
        in_specs=in_specs + [ANYWHERE] * (1 + len(held)),
        out_specs=[whole] * points,
        out_shape=[jax.ShapeDtypeStruct((slabs, 2, rows, columns), BF16)] * points,
        input_output_aliases={len(operands) + 1 + i: i for i in range(len(held))},
        scratch_shapes=[
            pltpu.VMEM((2, points, rows, columns), F32),
            pltpu.VMEM((2, points, rows, columns), F32),
            pltpu.VMEM((points, 2, rows, columns), F32),
        ],
        compiler_params=params(),
        cost_estimate=cost(),
        name="convolve",
    )(*operands, after, *held)
    return outs


def source_body(owners, *refs):
    pieces = refs[: len(owners)]
    g_ref, k_ref, b_ref, v_ref, sigma = refs[len(owners) :]
    me = lax.axis_index("energy")
    for piece, k in zip(pieces, owners):
        slabs, _, rows, _ = piece.shape
        start = pl.multiple_of((me ^ k) * rows, rows)
        for s in range(slabs):
            for part in range(2):
                sigma[s, part, pl.ds(start, rows), :] = piece[s, part]

    carry = None
    for s in range(sigma.shape[0]):
        left = jnp.concatenate([g_ref[0, s], g_ref[1, s]], axis=1)
        mixed = dot(left, panel(sigma[s, 0], sigma[s, 1])).astype(BF16)
        source = dot_nt(mixed, panel(g_ref[0, s], g_ref[1, s]))
        if carry is not None:
            high, low = k_ref[s, 0], k_ref[s, 1]
            source = times_adjoint(times_wide(high, low, carry), high, low) + source
        carry = source
        b_ref[s] = carry
    v_ref[...] = carry.astype(BF16)


def build_sources(pieces, green, kernels, energy, after):
    slabs, order = green.shape[2:4]
    return pl.pallas_call(
        ordered(functools.partial(source_body, range(len(pieces))), len(pieces) + 2),
        grid=(1,),
        in_specs=[pl.BlockSpec(x.shape, lambda i: (0, 0, 0, 0)) for x in pieces]
        + [
            pl.BlockSpec((2, None, slabs, order, order), lambda i: (0, energy, 0, 0, 0)),
            pl.BlockSpec((None, slabs, 2, order, 2 * order), lambda i: (energy, 0, 0, 0, 0)),
            ANYWHERE,
        ],
        out_specs=[
            pl.BlockSpec((slabs, order, 2 * order), lambda i: (0, 0, 0)),
            pl.BlockSpec((order, 2 * order), lambda i: (0, 0)),
        ],
        out_shape=[
            jax.ShapeDtypeStruct((slabs, order, 2 * order), F32),
            jax.ShapeDtypeStruct((order, 2 * order), BF16),
        ],
        scratch_shapes=[pltpu.VMEM((slabs, 2, order, order), BF16)],
        compiler_params=params(),
        cost_estimate=cost(),
        name="sources",
    )(*pieces, green, kernels, after)


def congruence(t_ref, x):
    order = x.shape[0]
    high, low = panels(t_ref)
    if x.dtype == F32:
        inner = times_wide(high, low, x)
    else:
        inner = times_narrow(high, low, x[:, :order], x[:, order:])
    return times_adjoint(inner, high, low)


def total(refs):
    value = refs[0][...]
    for ref in refs[1:]:
        value = value + ref[...]
    return value


def pair_body(v_ref, own_ref, sum_ref, t_ref, full_ref, short_ref):
    odd = (lax.axis_index("slab") & 1) == 1
    x = jnp.where(odd, v_ref[...], own_ref[...])
    base = jnp.where(odd, sum_ref[...], v_ref[...].astype(F32))
    value = base + congruence(t_ref, x)
    full_ref[...] = value
    short_ref[...] = value.astype(BF16)


def pair_sum(arrived, own, sums, maps, energy, *after):
    slabs, order, _ = sums.shape
    step, step_spec = one_map(maps, energy)
    whole = pl.BlockSpec((order, 2 * order), lambda i: (0, 0))
    return pl.pallas_call(
        ordered(pair_body, 4, len(after)),
        grid=(1,),
        in_specs=[whole, whole, pl.BlockSpec((None, order, 2 * order), lambda i: (slabs - 1, 0, 0)), step_spec]
        + [ANYWHERE] * len(after),
        out_specs=[whole] * 2,
        out_shape=[jax.ShapeDtypeStruct((order, 2 * order), t) for t in (F32, BF16)],
        compiler_params=params(),
        cost_estimate=cost(),
        name="pair_sum",
    )(arrived, own, sums, step, *after)


def combine(arrived, maps, base, energy, after):
    order = base.shape[0]
    step, step_spec = one_map(maps, energy)
    whole = pl.BlockSpec((order, 2 * order), lambda i: (0, 0))
    count = len(arrived)

    def body(*refs):
        t_ref, base_ref, _, out = refs[count:]
        out[...] = (base_ref[...] + congruence(t_ref, total(refs[:count]))).astype(BF16)

    return pl.pallas_call(
        body,
        grid=(1,),
        in_specs=[whole] * count + [step_spec, whole, ANYWHERE],
        out_specs=whole,
        out_shape=jax.ShapeDtypeStruct((order, 2 * order), BF16),
        compiler_params=params(),
        cost_estimate=cost(),
        name="combine",
    )(*arrived, step, base, after)


def keep(blocks, after):
    count = len(blocks)
    shape = (count,) + blocks[0].shape

    def body(*refs):
        for index in range(count):
            refs[-1][index] = refs[index][...]

    return pl.pallas_call(
        body,
        grid=(1,),
        in_specs=[pl.BlockSpec(shape[1:], lambda i: (0, 0))] * count + [ANYWHERE],
        out_specs=pl.BlockSpec(shape, lambda i: (0, 0, 0)),
        out_shape=jax.ShapeDtypeStruct(shape, BF16),
        compiler_params=params(),
        cost_estimate=cost(),
        name="keep",
    )(*blocks, after)


def finish_body(arrivals, ours, kept_ref, t_ref, m_ref, base_ref, out, entry):
    group, _, order, _ = m_ref.shape

    @pl.when(pl.program_id(0) == 0)
    def _():
        odd = (lax.axis_index("slab") & 1) == 1
        before = jnp.where(odd, ours[...].astype(F32) + kept_ref[...].astype(F32), 0.0)
        entry[...] = before + congruence(t_ref, total(arrivals))

    x_high, x_low = split(entry[...])
    xh = panel(x_high[:, :order], x_high[:, order:])
    xl = panel(x_low[:, :order], x_low[:, order:])
    both = dot(m_ref[...].reshape(group * 2 * order, 2 * order), xh)
    for index in range(group):
        first = 2 * index * order
        inner = both[first : first + order] + both[first + order : first + 2 * order] + dot(m_ref[index, 0], xl)
        value = times_adjoint(inner, m_ref[index, 0], m_ref[index, 1]) + base_ref[index]
        out[0, index] = value[:, :order]
        out[1, index] = value[:, order:]


def finish(arrived, ours, kept, inner, prefixes, sums, energy, held, after):
    energies, slabs, _, order, _ = prefixes.shape
    group = 2 if slabs % 2 == 0 else 1
    whole = pl.BlockSpec((order, 2 * order), lambda s: (0, 0))
    step, step_spec = one_map(inner, energy)
    operands = list(arrived) + [ours, kept, step, prefixes, sums, after]
    in_specs = [whole] * (len(arrived) + 1) + [
        pl.BlockSpec((None, order, 2 * order), lambda s: (energy, 0, 0)),
        step_spec,
        pl.BlockSpec((None, group, 2, order, 2 * order), lambda s: (energy, s, 0, 0, 0)),
        pl.BlockSpec((group, order, 2 * order), lambda s: (s, 0, 0)),
        ANYWHERE,
    ]
    aliases = {}
    if held is not None:
        aliases = {len(operands): 0}
        operands.append(held)
        in_specs.append(ANYWHERE)

    def body(*refs):
        fixed = refs[len(arrived) : len(arrived) + 5]
        finish_body(refs[: len(arrived)], *fixed, *refs[-2:])

    return pl.pallas_call(
        body,
        grid=(slabs // group,),
        in_specs=in_specs,
        out_specs=pl.BlockSpec((2, None, group, order, order), lambda s: (0, energy, s, 0, 0)),
        out_shape=jax.ShapeDtypeStruct((2, energies, slabs, order, order), F32),
        input_output_aliases=aliases,
        scratch_shapes=[pltpu.VMEM((order, 2 * order), F32)],
        compiler_params=params(),
        cost_estimate=cost(),
        name="finish",
    )(*operands)


def swap(x, k):
    count = lax.axis_size("energy")
    return lax.ppermute(x, "energy", [(i, i ^ k) for i in range(count)])


def other_of_pair(x):
    return lax.ppermute(x, "slab", [(i, i ^ 1) for i in range(lax.axis_size("slab"))])


def along(x, moves):
    count = lax.axis_size("energy")
    pairs = [(i * count + n, j * count + n) for n in range(count) for i, j in moves(n & 1)]
    return lax.ppermute(x, ("slab", "energy"), pairs)


def cut(slabs):
    return [(0, slabs - 1), (slabs - 1, 1)] if slabs > 1 else [(0, slabs)]


def per_device(green_lesser, screened_lesser, green_retarded, coupling):
    count = lax.axis_size("energy")
    depth = lax.axis_size("slab")
    if depth % 2 or count & (count - 1):
        raise ValueError("mesh axes")
    _, energies, slabs, order, _ = green_lesser.shape
    far = [k for k in range(count) if k >= 2]
    near = [k for k in range(min(2, count))]
    parts = cut(slabs)

    def first_rows(k, start, size):
        rows = order // count
        begin = (0, 0, start, (lax.axis_index("energy") ^ k) * rows, 0)
        sizes = (2, energies, size, rows, order)
        return [lax.dynamic_slice(x, begin, sizes) for x in (green_lesser, screened_lesser)]

    pieces = [[None] * count for _ in parts]
    for chunk, (start, size) in enumerate(parts):
        for k in far + near:
            block = jnp.stack(first_rows(k, start, size))
            pieces[chunk][k] = swap(block, k) if k else block
    token = pieces[0][0]

    kernels, prefixes = build_maps(green_retarded, coupling, token)
    token = kernels
    mine = [prefixes[e, slabs - 1] for e in range(energies)]
    other = [other_of_pair(x) for x in mine]

    blocks = ()
    for chunk, (start, size) in enumerate(parts):
        if chunk == len(parts) - 1:
            pair_step, plane, inner = pair_maps(mine, other, energies, token)
            token = plane
        blocks = convolve(pieces[chunk], start, slabs, size, blocks, token)
        token = blocks[0]
    sigma = [[None] * count for _ in range(energies)]
    for e in range(energies):
        for k in range(count):
            block = blocks[k * energies + e]
            sigma[e][k] = swap(block, k) if k else block

    pairs = depth // 2
    sums, own, ours = ([None] * energies for _ in range(3))
    running, carry = [None] * energies, [None] * energies
    arrived = [[] for _ in range(energies)]

    def to_carrier(lane):
        return [(2 * z + 1 - lane, 2 * z + lane) for z in range(pairs)]

    def to_second(lane):
        return [(2 * z, 2 * z + 1) for z in range(pairs)] if lane == 0 else []

    def onward(step):
        def moves(lane):
            ahead = [(2 * step + lane, 2 * step + 2 + lane)] if step < pairs - 1 else []
            aside = [(2 * step - 2 + lane, 2 * step + 1 - lane)] if step > 0 else []
            return ahead + aside

        return moves

    kept = None

    def stage(e, step):
        nonlocal token, kept
        if step == 0:
            sums[e], own[e] = build_sources(sigma[e], green_retarded, kernels, e, token)
            token = own[e]
            ours[e] = along(own[e], to_carrier)
        elif step == 1:
            running[e], carry[e] = pair_sum(ours[e], own[e], sums[e], pair_step, e, token)
            token = carry[e]
            arrived[e].append(along(carry[e], onward(0)))
            if e == energies - 1:
                token = keep(own, token)
                kept = along(token, to_second)
        else:
            carry[e] = token = combine(arrived[e], plane, running[e], e, token)
            arrived[e].append(along(carry[e], onward(step - 1)))
        if step == last:
            arrived[e].append(along(carry[e], onward(pairs - 1)))

    last = max(pairs - 1, 1)
    for step in range(last + 1):
        for e in range(energies):
            stage(e, step)
    result = None
    for e in range(energies):
        result = finish(arrived[e], ours[e], kept, inner, prefixes, sums[e], e, result, token)
    return result


def solution(mesh):
    placed = (
        P(None, "energy", "slab", None, None),
        P(None, "energy", "slab", None, None),
        P(None, "energy", "slab", None, None),
        P(None, "slab", None, None),
    )
    return jax.shard_map(
        per_device,
        mesh=mesh,
        in_specs=placed,
        out_specs=P(None, "energy", "slab", None, None),
        check_vma=False,
    )
```

```python
import functools

import jax
import jax.numpy as jnp
from jax import lax
from jax.experimental import pallas as pl
from jax.experimental.pallas import tpu as pltpu
from jax.sharding import PartitionSpec as P

BF16 = jnp.bfloat16
F32 = jnp.float32
VMEM_LIMIT = 24 * 1024 * 1024


def params():
    return pltpu.CompilerParams(vmem_limit_bytes=VMEM_LIMIT)


def ordered(body, count, extra=1):
    def run(*refs):
        body(*refs[:count], *refs[count + extra :])

    return run


ANYWHERE = pl.BlockSpec(memory_space=pl.ANY)


def cost():
    return pl.CostEstimate(flops=0, bytes_accessed=0, transcendentals=0)


def split(value):
    high = value.astype(BF16)
    low = (value - high.astype(F32)).astype(BF16)
    return high, low


def panel(re, im):
    return jnp.concatenate(
        [jnp.concatenate([re, im], axis=1), jnp.concatenate([-im, re], axis=1)], axis=0
    )


def dot(left, right):
    return lax.dot_general(left, right, (((1,), (0,)), ((), ())), preferred_element_type=F32)


def dot_nt(left, right):
    return lax.dot_general(left, right, (((1,), (1,)), ((), ())), preferred_element_type=F32)


def times_wide(a_high, a_low, x):
    order = x.shape[0]
    x_high, x_low = split(x)
    xh = panel(x_high[:, :order], x_high[:, order:])
    xl = panel(x_low[:, :order], x_low[:, order:])
    left = jnp.concatenate([a_high, a_high, a_low], axis=1)
    return dot(left, jnp.concatenate([xh, xl, xh], axis=0))


def times_narrow(a_high, a_low, re, im):
    xp = panel(re, im)
    left = jnp.concatenate([a_high, a_low], axis=1)
    return dot(left, jnp.concatenate([xp, xp], axis=0))


def times_adjoint(y, t_high, t_low):
    order = y.shape[0]
    y_high, y_low = split(y)
    th = panel(t_high[:, :order], t_high[:, order:])
    tl = panel(t_low[:, :order], t_low[:, order:])
    left = jnp.concatenate([y_high, y_low, y_high], axis=1)
    return dot_nt(left, jnp.concatenate([th, th, tl], axis=1))


def panels(ref):
    return ref[0], ref[1]


def store_map(ref, value):
    high, low = split(value)
    ref[0] = high
    ref[1] = low


def pack_body(wanted, *refs):
    sources, outs, sems = refs[:2], refs[-1 - len(wanted) : -1], refs[-1]
    copies = []
    for out, (parts, k, start) in zip(outs, wanted):
        size, rows = out.shape[-4 + 1 : -1]
        begin = pl.multiple_of((lax.axis_index("energy") ^ k) * rows, rows)
        for part in parts:
            block = sources[part].at[:, :, pl.ds(start, size), pl.ds(begin, rows), :]
            target = out if len(parts) == 1 else out.at[part]
            copies.append(pltpu.make_async_copy(block, target, sems.at[len(copies)]))
    for copy in copies:
        copy.start()
    for copy in copies:
        copy.wait()


def pack(green, screen, wanted, count, *after):
    _, energies, _, order, _ = green.shape
    shapes = [
        (len(parts),) * (len(parts) > 1) + (2, energies, size, order // count, order)
        for parts, _, _, size in wanted
    ]
    return pl.pallas_call(
        functools.partial(pack_body, [w[:3] for w in wanted]),
        in_specs=[ANYWHERE] * (2 + len(after)),
        out_specs=[pl.BlockSpec(memory_space=pltpu.VMEM)] * len(wanted),
        out_shape=[jax.ShapeDtypeStruct(shape, BF16) for shape in shapes],
        scratch_shapes=[pltpu.SemaphoreType.DMA((sum(len(w[0]) for w in wanted),))],
        compiler_params=params(),
        cost_estimate=cost(),
        name="pack",
    )(green, screen, *after)


def maps_body(g_ref, c_ref, k_ref, p_ref, carry):
    left = jnp.concatenate([g_ref[0], g_ref[1]], axis=1)
    value = dot(left, panel(c_ref[0], c_ref[1]))
    store_map(k_ref, value)

    @pl.when(pl.program_id(1) == 0)
    def _():
        carry[...] = value

    @pl.when(pl.program_id(1) > 0)
    def _():
        high, low = panels(k_ref)
        carry[...] = times_wide(high, low, carry[...])

    store_map(p_ref, carry[...])


def build_maps(green, coupling, *after):
    _, energies, slabs, order, _ = green.shape
    shape = jax.ShapeDtypeStruct((energies, slabs, 2, order, 2 * order), BF16)
    out_spec = pl.BlockSpec((None, None, 2, order, 2 * order), lambda e, s: (e, s, 0, 0, 0))
    return pl.pallas_call(
        lambda *refs: maps_body(*refs[:2], *refs[2 + len(after) :]),
        grid=(energies, slabs),
        in_specs=[
            pl.BlockSpec((2, None, None, order, order), lambda e, s: (0, e, s, 0, 0)),
            pl.BlockSpec((2, None, order, order), lambda e, s: (0, s, 0, 0)),
        ]
        + [ANYWHERE] * len(after),
        out_specs=[out_spec, out_spec],
        out_shape=[shape, shape],
        scratch_shapes=[pltpu.VMEM((order, 2 * order), F32)],
        compiler_params=params(),
        cost_estimate=cost(),
        name="maps",
    )(green, coupling, *after)


def one_map(maps, energy):
    if isinstance(maps, list):
        return maps[energy], pl.BlockSpec(maps[energy].shape, lambda *_: (0, 0, 0))
    return maps, pl.BlockSpec((None,) + maps.shape[1:], lambda *_: (energy, 0, 0, 0))


def pair_maps_body(energies, *refs):
    step, plane, inner = refs[-3:]
    odd = (lax.axis_index("slab") & 1) == 1
    for e in range(energies):
        mine, other = refs[2 * e], refs[2 * e + 1]
        order = mine.shape[1]
        first = [jnp.where(odd, mine[part], other[part]) for part in range(2)]
        second = [jnp.where(odd, other[part], mine[part]).astype(F32) for part in range(2)]
        store_map(plane.at[e], times_wide(*first, second[0] + second[1]))
        row = lax.broadcasted_iota(jnp.int32, (order, 2 * order), 0)
        column = lax.broadcasted_iota(jnp.int32, (order, 2 * order), 1)
        unit = jnp.where(row == column, 1.0, 0.0)
        for part in range(2):
            step[e, part] = first[part]
            identity = unit if part == 0 else jnp.zeros_like(unit)
            inner[e, part] = jnp.where(odd, other[part].astype(F32), identity).astype(BF16)


def pair_maps(mine, other, energies, after):
    pairs = [one_map(maps, e) for e in range(energies) for maps in (mine, other)]
    shape = (energies,) + pairs[0][1].block_shape[-3:]
    return pl.pallas_call(
        ordered(functools.partial(pair_maps_body, energies), 2 * energies),
        grid=(1,),
        in_specs=[spec for _, spec in pairs] + [ANYWHERE],
        out_specs=[pl.BlockSpec(shape, lambda i: (0, 0, 0, 0))] * 3,
        out_shape=[jax.ShapeDtypeStruct(shape, BF16)] * 3,
        compiler_params=params(),
        cost_estimate=cost(),
        name="pair_maps",
    )(*[maps for maps, _ in pairs], after)


def convolve_body(pairs, energies, shared, *refs):
    count = len(pairs)
    taken = sum(1 + pair for pair in pairs)
    ins, outs = list(refs[:taken]), refs[taken + 1 + shared :]
    green, screen, total = refs[-3:]
    me = lax.axis_index("energy")
    points = count * energies
    middle = points // 2
    rows, columns = green.shape[2:]
    for k in range(count):
        base = (me ^ k) * energies
        piece = ins.pop(0)
        halves = (piece, ins.pop(0)) if pairs[k] else (piece.at[0], piece.at[1])
        for e in range(energies):
            green[:, base + e] = halves[0][:, e].astype(F32)
            screen[:, base + e] = halves[1][:, e].astype(F32)

    def tile(index, _):
        row = pl.multiple_of(index * 8, 8)
        for col in range(0, columns, 128):
            at = (pl.ds(row, 8), pl.ds(col, 128))
            gr = [green[(0, m) + at] for m in range(points)]
            gi = [green[(1, m) + at] for m in range(points)]
            wr = [screen[(0, m) + at] for m in range(points)]
            wi = [screen[(1, m) + at] for m in range(points)]
            for n in range(points):
                re = None
                im = None
                for m in range(points):
                    lag = n - m + middle
                    if 0 <= lag < points:
                        a = gr[m] * wr[lag] - gi[m] * wi[lag]
                        b = gr[m] * wi[lag] + gi[m] * wr[lag]
                        re = a if re is None else re + a
                        im = b if im is None else im + b
                total[(n, 0) + at] = -im / points
                total[(n, 1) + at] = re / points
        return 0

    lax.fori_loop(0, rows // 8, tile, 0)
    for k in range(count):
        base = (me ^ k) * energies
        for e in range(energies):
            outs[k * energies + e][...] = total[base + e].astype(BF16)


def convolve(pieces, start, slabs, size, held, after):
    count = len(pieces)
    pairs = [isinstance(piece, tuple) for piece in pieces]
    operands, in_specs = [], []
    for piece, pair in zip(pieces, pairs):
        if pair:
            operands += piece
            energies, _, rows, columns = piece[0].shape[1:]
            in_specs += [pl.BlockSpec((2, energies, None, rows, columns), lambda s: (0, 0, s + start, 0, 0))] * 2
        else:
            operands.append(piece)
            energies, _, rows, columns = piece.shape[2:]
            first = start if piece.shape[3] == slabs else 0
            block = (2, 2, energies, None, rows, columns)
            in_specs.append(pl.BlockSpec(block, lambda s, first=first: (0, 0, 0, s + first, 0, 0)))
    points = count * energies
    whole = pl.BlockSpec((None, 2, rows, columns), lambda s: (s + start, 0, 0, 0))
    outs = pl.pallas_call(
        functools.partial(convolve_body, pairs, energies, len(held)),
        grid=(size,),
        in_specs=in_specs + [ANYWHERE] * (1 + len(held)),
        out_specs=[whole] * points,
        out_shape=[jax.ShapeDtypeStruct((slabs, 2, rows, columns), BF16)] * points,
        input_output_aliases={len(operands) + 1 + i: i for i in range(len(held))},
        scratch_shapes=[
            pltpu.VMEM((2, points, rows, columns), F32),
            pltpu.VMEM((2, points, rows, columns), F32),
            pltpu.VMEM((points, 2, rows, columns), F32),
        ],
        compiler_params=params(),
        cost_estimate=cost(),
        name="convolve",
    )(*operands, after, *held)
    return outs


def source_body(owners, *refs):
    pieces = refs[: len(owners)]
    g_ref, k_ref, b_ref, v_ref, sigma = refs[len(owners) :]
    me = lax.axis_index("energy")
    for piece, k in zip(pieces, owners):
        slabs, _, rows, _ = piece.shape
        start = pl.multiple_of((me ^ k) * rows, rows)
        for s in range(slabs):
            for part in range(2):
                sigma[s, part, pl.ds(start, rows), :] = piece[s, part]

    carry = None
    for s in range(sigma.shape[0]):
        left = jnp.concatenate([g_ref[0, s], g_ref[1, s]], axis=1)
        mixed = dot(left, panel(sigma[s, 0], sigma[s, 1])).astype(BF16)
        source = dot_nt(mixed, panel(g_ref[0, s], g_ref[1, s]))
        if carry is not None:
            high, low = k_ref[s, 0], k_ref[s, 1]
            source = times_adjoint(times_wide(high, low, carry), high, low) + source
        carry = source
        b_ref[s] = carry
    v_ref[...] = carry.astype(BF16)


def build_sources(pieces, green, kernels, energy, after):
    slabs, order = green.shape[2:4]
    owners = [k for k in range(len(pieces)) if k >= 2] + [k for k in (1, 0) if k < len(pieces)]
    pieces = [pieces[k] for k in owners]
    return pl.pallas_call(
        ordered(functools.partial(source_body, owners), len(pieces) + 2),
        grid=(1,),
        in_specs=[pl.BlockSpec(x.shape, lambda i: (0, 0, 0, 0)) for x in pieces]
        + [
            pl.BlockSpec((2, None, slabs, order, order), lambda i: (0, energy, 0, 0, 0)),
            pl.BlockSpec((None, slabs, 2, order, 2 * order), lambda i: (energy, 0, 0, 0, 0)),
            ANYWHERE,
        ],
        out_specs=[
            pl.BlockSpec((slabs, order, 2 * order), lambda i: (0, 0, 0)),
            pl.BlockSpec((order, 2 * order), lambda i: (0, 0)),
        ],
        out_shape=[
            jax.ShapeDtypeStruct((slabs, order, 2 * order), F32),
            jax.ShapeDtypeStruct((order, 2 * order), BF16),
        ],
        scratch_shapes=[pltpu.VMEM((slabs, 2, order, order), BF16)],
        compiler_params=params(),
        cost_estimate=cost(),
        name="sources",
    )(*pieces, green, kernels, after)


def congruence(t_ref, x):
    order = x.shape[0]
    high, low = panels(t_ref)
    if x.dtype == F32:
        inner = times_wide(high, low, x)
    else:
        inner = times_narrow(high, low, x[:, :order], x[:, order:])
    return times_adjoint(inner, high, low)


def total(refs):
    value = refs[0][...]
    for ref in refs[1:]:
        value = value + ref[...]
    return value


def pair_body(v_ref, own_ref, sum_ref, t_ref, full_ref, short_ref):
    odd = (lax.axis_index("slab") & 1) == 1
    theirs = v_ref[...]
    x = jnp.where(odd, theirs, own_ref[...])
    base = jnp.where(odd, sum_ref[...], theirs.astype(F32))
    value = base + congruence(t_ref, x)
    full_ref[...] = value
    short_ref[...] = value.astype(BF16)


def pair_sum(arrived, own, sums, maps, energy, *after):
    slabs, order, _ = sums.shape
    step, step_spec = one_map(maps, energy)
    whole = pl.BlockSpec((order, 2 * order), lambda i: (0, 0))
    return pl.pallas_call(
        ordered(pair_body, 4, len(after)),
        grid=(1,),
        in_specs=[whole, whole, pl.BlockSpec((None, order, 2 * order), lambda i: (slabs - 1, 0, 0)), step_spec]
        + [ANYWHERE] * len(after),
        out_specs=[whole] * 2,
        out_shape=[jax.ShapeDtypeStruct((order, 2 * order), t) for t in (F32, BF16)],
        compiler_params=params(),
        cost_estimate=cost(),
        name="pair_sum",
    )(arrived, own, sums, step, *after)


def combine(arrived, maps, base, energy, after):
    order = base.shape[0]
    step, step_spec = one_map(maps, energy)
    whole = pl.BlockSpec((order, 2 * order), lambda i: (0, 0))
    count = len(arrived)

    def body(*refs):
        t_ref, base_ref, _, out = refs[count:]
        out[...] = (base_ref[...] + congruence(t_ref, total(refs[:count]))).astype(BF16)

    return pl.pallas_call(
        body,
        grid=(1,),
        in_specs=[whole] * count + [step_spec, whole, ANYWHERE],
        out_specs=whole,
        out_shape=jax.ShapeDtypeStruct((order, 2 * order), BF16),
        compiler_params=params(),
        cost_estimate=cost(),
        name="combine",
    )(*arrived, step, base, after)


def keep(block, after):
    def body(source, _, out):
        out[...] = source[...]

    whole = pl.BlockSpec(block.shape, lambda i: (0, 0))
    return pl.pallas_call(
        body,
        grid=(1,),
        in_specs=[whole, ANYWHERE],
        out_specs=whole,
        out_shape=jax.ShapeDtypeStruct(block.shape, BF16),
        compiler_params=params(),
        cost_estimate=cost(),
        name="keep",
    )(block, after)


def finish_body(arrivals, ours_ref, kept_ref, t_ref, m_ref, base_ref, out, entry):
    group, _, order, _ = m_ref.shape

    @pl.when(pl.program_id(0) == 0)
    def _():
        odd = (lax.axis_index("slab") & 1) == 1
        before = jnp.where(odd, ours_ref[...].astype(F32) + kept_ref[...].astype(F32), 0.0)
        entry[...] = (before + congruence(t_ref, total(arrivals))).astype(BF16)

    both = dot(m_ref[...].reshape(group * 2 * order, 2 * order), panel(entry[:, :order], entry[:, order:]))
    for index in range(group):
        first = 2 * index * order
        inner = both[first : first + order] + both[first + order : first + 2 * order]
        value = times_adjoint(inner, m_ref[index, 0], m_ref[index, 1]) + base_ref[index]
        out[0, index] = value[:, :order]
        out[1, index] = value[:, order:]


def finish(arrived, ours, kept, inner, prefixes, sums, energy, held, after):
    energies, slabs, _, order, _ = prefixes.shape
    group = 2 if slabs % 2 == 0 else 1
    whole = pl.BlockSpec((order, 2 * order), lambda s: (0, 0))
    step, step_spec = one_map(inner, energy)
    operands = list(arrived) + [ours, kept, step, prefixes, sums, after]
    in_specs = [whole] * (len(arrived) + 2) + [
        step_spec,
        pl.BlockSpec((None, group, 2, order, 2 * order), lambda s: (energy, s, 0, 0, 0)),
        pl.BlockSpec((group, order, 2 * order), lambda s: (s, 0, 0)),
        ANYWHERE,
    ]
    aliases = {}
    if held is not None:
        aliases = {len(operands): 0}
        operands.append(held)
        in_specs.append(ANYWHERE)

    def body(*refs):
        finish_body(refs[: len(arrived)], *refs[len(arrived) : len(arrived) + 5], *refs[-2:])

    return pl.pallas_call(
        body,
        grid=(slabs // group,),
        in_specs=in_specs,
        out_specs=pl.BlockSpec((2, None, group, order, order), lambda s: (0, energy, s, 0, 0)),
        out_shape=jax.ShapeDtypeStruct((2, energies, slabs, order, order), F32),
        input_output_aliases=aliases,
        scratch_shapes=[pltpu.VMEM((order, 2 * order), BF16)],
        compiler_params=params(),
        cost_estimate=cost(),
        name="finish",
    )(*operands)


def swap(x, k):
    count = lax.axis_size("energy")
    return lax.ppermute(x, "energy", [(i, i ^ k) for i in range(count)])


def other_of_pair(x):
    return lax.ppermute(x, "slab", [(i, i ^ 1) for i in range(lax.axis_size("slab"))])


def along(x, moves):
    count = lax.axis_size("energy")
    pairs = [(i * count + n, j * count + n) for n in range(count) for i, j in moves(n & 1)]
    return lax.ppermute(x, ("slab", "energy"), pairs)


def cut(slabs):
    return [(0, slabs - 1), (slabs - 1, 1)] if slabs > 1 else [(0, slabs)]


def per_device(green_lesser, screened_lesser, green_retarded, coupling):
    count = lax.axis_size("energy")
    depth = lax.axis_size("slab")
    if depth % 2 or count & (count - 1):
        raise ValueError("mesh axes")
    _, energies, slabs, order, _ = green_lesser.shape
    far = [k for k in range(count) if k >= 2]
    near = [k for k in range(min(2, count))]
    parts = cut(slabs)

    def first_rows(k, start, size):
        rows = order // count
        begin = (0, 0, start, (lax.axis_index("energy") ^ k) * rows, 0)
        sizes = (2, energies, size, rows, order)
        return [lax.dynamic_slice(x, begin, sizes) for x in (green_lesser, screened_lesser)]

    pieces = [[None] * count for _ in parts]
    for chunk, (start, size) in enumerate(parts):
        for k in far + near:
            block = jnp.stack(first_rows(k, start, size))
            pieces[chunk][k] = swap(block, k) if k else block
    token = pieces[0][0]

    kernels, prefixes = build_maps(green_retarded, coupling, token)
    token = kernels
    mine = [prefixes[e, slabs - 1] for e in range(energies)]
    other = [other_of_pair(x) for x in mine]

    blocks = ()
    for chunk, (start, size) in enumerate(parts):
        if chunk == len(parts) - 1:
            pair_step, plane, inner = pair_maps(mine, other, energies, token)
            token = plane
        blocks = convolve(pieces[chunk], start, slabs, size, blocks, token)
        token = blocks[0]
    sigma = [[None] * count for _ in range(energies)]
    for e in range(energies):
        for k in range(count):
            block = blocks[k * energies + e]
            sigma[e][k] = swap(block, k) if k else block

    pairs = depth // 2
    sums, own, ours = ([None] * energies for _ in range(3))
    running, carry = [None] * energies, [None] * energies
    arrived = [[] for _ in range(energies)]

    def to_carrier(lane):
        return [(2 * z + 1 - lane, 2 * z + lane) for z in range(pairs)]

    def to_second(lane):
        return [(2 * z, 2 * z + 1) for z in range(pairs)] if lane == 0 else []

    def onward(step):
        def moves(lane):
            ahead = [(2 * step + lane, 2 * step + 2 + lane)] if step < pairs - 1 else []
            aside = [(2 * step - 2 + lane, 2 * step + 1 - lane)] if step > 0 else []
            return ahead + aside

        return moves

    kept = [None] * energies

    def stage(e, step):
        nonlocal token
        if step == 0:
            sums[e], own[e] = build_sources(sigma[e], green_retarded, kernels, e, token)
            token = own[e]
            ours[e] = along(own[e], to_carrier)
            if e < energies - 1:
                kept[e] = along(own[e], to_second)
        elif step == 1:
            early = [kept[e]] if kept[e] is not None else []
            running[e], carry[e] = pair_sum(ours[e], own[e], sums[e], pair_step, e, token, *early)
            token = carry[e]
            arrived[e].append(along(carry[e], onward(0)))
            if e == energies - 1:
                token = keep(own[e], token)
                kept[e] = along(token, to_second)
        else:
            carry[e] = token = combine(arrived[e], plane, running[e], e, token)
            arrived[e].append(along(carry[e], onward(step - 1)))
        if step == last:
            arrived[e].append(along(carry[e], onward(pairs - 1)))

    last = max(pairs - 1, 1)
    for step in range(last + 1):
        for e in range(energies):
            stage(e, step)
    result = None
    for e in range(energies):
        result = finish(arrived[e], ours[e], kept[e], inner, prefixes, sums[e], e, result, token)
    return result


def solution(mesh):
    placed = (
        P(None, "energy", "slab", None, None),
        P(None, "energy", "slab", None, None),
        P(None, "energy", "slab", None, None),
        P(None, "slab", None, None),
    )
    return jax.shard_map(
        per_device,
        mesh=mesh,
        in_specs=placed,
        out_specs=P(None, "energy", "slab", None, None),
        check_vma=False,
    )
```

```python
import functools

import jax
import jax.numpy as jnp
from jax import lax
from jax.experimental import pallas as pl
from jax.experimental.pallas import tpu as pltpu
from jax.sharding import PartitionSpec as P

BF16 = jnp.bfloat16
F32 = jnp.float32
VMEM_LIMIT = 24 * 1024 * 1024


def params():
    return pltpu.CompilerParams(vmem_limit_bytes=VMEM_LIMIT)


def ordered(body, count, extra=1):
    def run(*refs):
        body(*refs[:count], *refs[count + extra :])

    return run


ANYWHERE = pl.BlockSpec(memory_space=pl.ANY)
WHOLE = pl.BlockSpec(memory_space=pltpu.VMEM)


def cost():
    return pl.CostEstimate(flops=0, bytes_accessed=0, transcendentals=0)


def split(value):
    high = value.astype(BF16)
    low = (value - high.astype(F32)).astype(BF16)
    return high, low


def panel(re, im):
    return jnp.concatenate(
        [jnp.concatenate([re, im], axis=1), jnp.concatenate([-im, re], axis=1)], axis=0
    )


def dot(left, right):
    return lax.dot_general(left, right, (((1,), (0,)), ((), ())), preferred_element_type=F32)


def dot_nt(left, right):
    return lax.dot_general(left, right, (((1,), (1,)), ((), ())), preferred_element_type=F32)


def times_wide(a_high, a_low, x):
    order = x.shape[0]
    x_high, x_low = split(x)
    xh = panel(x_high[:, :order], x_high[:, order:])
    xl = panel(x_low[:, :order], x_low[:, order:])
    left = jnp.concatenate([a_high, a_high, a_low], axis=1)
    return dot(left, jnp.concatenate([xh, xl, xh], axis=0))


def times_narrow(a_high, a_low, re, im):
    xp = panel(re, im)
    left = jnp.concatenate([a_high, a_low], axis=1)
    return dot(left, jnp.concatenate([xp, xp], axis=0))


def times_adjoint(y, t_high, t_low):
    order = y.shape[0]
    y_high, y_low = split(y)
    th = panel(t_high[:, :order], t_high[:, order:])
    tl = panel(t_low[:, :order], t_low[:, order:])
    left = jnp.concatenate([y_high, y_low, y_high], axis=1)
    return dot_nt(left, jnp.concatenate([th, th, tl], axis=1))


def panels(ref):
    return ref[0], ref[1]


def store_map(ref, value):
    high, low = split(value)
    ref[0] = high
    ref[1] = low


def pack_body(wanted, *refs):
    sources, outs, sems = refs[:2], refs[-1 - len(wanted) : -1], refs[-1]
    copies = []
    for out, (parts, k, start) in zip(outs, wanted):
        size, rows = out.shape[-4 + 1 : -1]
        begin = pl.multiple_of((lax.axis_index("energy") ^ k) * rows, rows)
        for part in parts:
            block = sources[part].at[:, :, pl.ds(start, size), pl.ds(begin, rows), :]
            target = out if len(parts) == 1 else out.at[part]
            copies.append(pltpu.make_async_copy(block, target, sems.at[len(copies)]))
    for copy in copies:
        copy.start()
    for copy in copies:
        copy.wait()


def pack(green, screen, wanted, count, *after):
    _, energies, _, order, _ = green.shape
    shapes = [
        (len(parts),) * (len(parts) > 1) + (2, energies, size, order // count, order)
        for parts, _, _, size in wanted
    ]
    return pl.pallas_call(
        functools.partial(pack_body, [w[:3] for w in wanted]),
        in_specs=[ANYWHERE] * (2 + len(after)),
        out_specs=[pl.BlockSpec(memory_space=pltpu.VMEM)] * len(wanted),
        out_shape=[jax.ShapeDtypeStruct(shape, BF16) for shape in shapes],
        scratch_shapes=[pltpu.SemaphoreType.DMA((sum(len(w[0]) for w in wanted),))],
        compiler_params=params(),
        cost_estimate=cost(),
        name="pack",
    )(green, screen, *after)


def maps_body(g_ref, c_ref, k_ref, p_ref, carry):
    left = jnp.concatenate([g_ref[0], g_ref[1]], axis=1)
    value = dot(left, panel(c_ref[0], c_ref[1]))
    store_map(k_ref, value)

    @pl.when(pl.program_id(1) == 0)
    def _():
        carry[...] = value

    @pl.when(pl.program_id(1) > 0)
    def _():
        high, low = panels(k_ref)
        carry[...] = times_wide(high, low, carry[...])

    store_map(p_ref, carry[...])


def build_maps(green, coupling, *after):
    _, energies, slabs, order, _ = green.shape
    shape = jax.ShapeDtypeStruct((energies, slabs, 2, order, 2 * order), BF16)
    out_spec = pl.BlockSpec((None, None, 2, order, 2 * order), lambda e, s: (e, s, 0, 0, 0))
    return pl.pallas_call(
        lambda *refs: maps_body(*refs[:2], *refs[2 + len(after) :]),
        grid=(energies, slabs),
        in_specs=[
            pl.BlockSpec((2, None, None, order, order), lambda e, s: (0, e, s, 0, 0)),
            pl.BlockSpec((2, None, order, order), lambda e, s: (0, s, 0, 0)),
        ]
        + [ANYWHERE] * len(after),
        out_specs=[out_spec, out_spec],
        out_shape=[shape, shape],
        scratch_shapes=[pltpu.VMEM((order, 2 * order), F32)],
        compiler_params=params(),
        cost_estimate=cost(),
        name="maps",
    )(green, coupling, *after)


def one_map(maps, energy):
    if isinstance(maps, list):
        return maps[energy], pl.BlockSpec(maps[energy].shape, lambda *_: (0, 0, 0))
    return maps, pl.BlockSpec((None,) + maps.shape[1:], lambda *_: (energy, 0, 0, 0))


def pair_maps_body(energies, *refs):
    step, plane, inner = refs[-3:]
    odd = (lax.axis_index("slab") & 1) == 1
    for e in range(energies):
        mine, other = refs[2 * e], refs[2 * e + 1]
        order = mine.shape[1]
        first = [jnp.where(odd, mine[part], other[part]) for part in range(2)]
        second = [jnp.where(odd, other[part], mine[part]).astype(F32) for part in range(2)]
        store_map(plane.at[e], times_wide(*first, second[0] + second[1]))
        row = lax.broadcasted_iota(jnp.int32, (order, 2 * order), 0)
        column = lax.broadcasted_iota(jnp.int32, (order, 2 * order), 1)
        unit = jnp.where(row == column, 1.0, 0.0)
        for part in range(2):
            step[e, part] = first[part]
            identity = unit if part == 0 else jnp.zeros_like(unit)
            inner[e, part] = jnp.where(odd, other[part].astype(F32), identity).astype(BF16)


def pair_maps(mine, other, energies, after):
    pairs = [one_map(maps, e) for e in range(energies) for maps in (mine, other)]
    shape = (energies,) + pairs[0][1].block_shape[-3:]
    return pl.pallas_call(
        ordered(functools.partial(pair_maps_body, energies), 2 * energies),
        grid=(1,),
        in_specs=[spec for _, spec in pairs] + [ANYWHERE],
        out_specs=[pl.BlockSpec(shape, lambda i: (0, 0, 0, 0))] * 3,
        out_shape=[jax.ShapeDtypeStruct(shape, BF16)] * 3,
        compiler_params=params(),
        cost_estimate=cost(),
        name="pair_maps",
    )(*[maps for maps, _ in pairs], after)


def convolve_body(pairs, energies, shared, *refs):
    count = len(pairs)
    taken = sum(1 + pair for pair in pairs)
    ins, outs = list(refs[:taken]), refs[taken + 1 + shared :]
    green, screen, total = refs[-3:]
    me = lax.axis_index("energy")
    points = count * energies
    middle = points // 2
    rows, columns = green.shape[2:]
    for k in range(count):
        base = (me ^ k) * energies
        piece = ins.pop(0)
        halves = (piece, ins.pop(0)) if pairs[k] else (piece.at[0], piece.at[1])
        for e in range(energies):
            green[:, base + e] = halves[0][:, e].astype(F32)
            screen[:, base + e] = halves[1][:, e].astype(F32)

    def tile(index, _):
        row = pl.multiple_of(index * 8, 8)
        for col in range(0, columns, 128):
            at = (pl.ds(row, 8), pl.ds(col, 128))
            gr = [green[(0, m) + at] for m in range(points)]
            gi = [green[(1, m) + at] for m in range(points)]
            wr = [screen[(0, m) + at] for m in range(points)]
            wi = [screen[(1, m) + at] for m in range(points)]
            for n in range(points):
                re = None
                im = None
                for m in range(points):
                    lag = n - m + middle
                    if 0 <= lag < points:
                        a = gr[m] * wr[lag] - gi[m] * wi[lag]
                        b = gr[m] * wi[lag] + gi[m] * wr[lag]
                        re = a if re is None else re + a
                        im = b if im is None else im + b
                total[(n, 0) + at] = -im / points
                total[(n, 1) + at] = re / points
        return 0

    lax.fori_loop(0, rows // 8, tile, 0)
    for k in range(count):
        base = (me ^ k) * energies
        for e in range(energies):
            outs[k * energies + e][...] = total[base + e].astype(BF16)


def convolve(pieces, start, slabs, size, held, after):
    count = len(pieces)
    pairs = [isinstance(piece, tuple) for piece in pieces]
    operands, in_specs = [], []
    for piece, pair in zip(pieces, pairs):
        if pair:
            operands += piece
            energies, _, rows, columns = piece[0].shape[1:]
            in_specs += [pl.BlockSpec((2, energies, None, rows, columns), lambda s: (0, 0, s + start, 0, 0))] * 2
        else:
            operands.append(piece)
            energies, _, rows, columns = piece.shape[2:]
            first = start if piece.shape[3] == slabs else 0
            block = (2, 2, energies, None, rows, columns)
            in_specs.append(pl.BlockSpec(block, lambda s, first=first: (0, 0, 0, s + first, 0, 0)))
    points = count * energies
    whole = pl.BlockSpec((None, 2, rows, columns), lambda s: (s + start, 0, 0, 0))
    outs = pl.pallas_call(
        functools.partial(convolve_body, pairs, energies, len(held)),
        grid=(size,),
        in_specs=in_specs + [ANYWHERE] * (1 + len(held)),
        out_specs=[whole] * points,
        out_shape=[jax.ShapeDtypeStruct((slabs, 2, rows, columns), BF16)] * points,
        input_output_aliases={len(operands) + 1 + i: i for i in range(len(held))},
        scratch_shapes=[
            pltpu.VMEM((2, points, rows, columns), F32),
            pltpu.VMEM((2, points, rows, columns), F32),
            pltpu.VMEM((points, 2, rows, columns), F32),
        ],
        compiler_params=params(),
        cost_estimate=cost(),
        name="convolve",
    )(*operands, after, *held)
    return outs


def source_body(energy, owners, *refs):
    pieces = refs[: len(owners)]
    g_ref, k_ref, b_ref, v_ref, sigma = refs[len(owners) :]
    me = lax.axis_index("energy")
    for piece, k in zip(pieces, owners):
        slabs, _, rows, _ = piece.shape
        start = pl.multiple_of((me ^ k) * rows, rows)
        for s in range(slabs):
            for part in range(2):
                sigma[s, part, pl.ds(start, rows), :] = piece[s, part]

    carry = None
    for s in range(sigma.shape[0]):
        green_re, green_im = g_ref[0, energy, s], g_ref[1, energy, s]
        left = jnp.concatenate([green_re, green_im], axis=1)
        mixed = dot(left, panel(sigma[s, 0], sigma[s, 1])).astype(BF16)
        source = dot_nt(mixed, panel(green_re, green_im))
        if carry is not None:
            high, low = k_ref[energy, s, 0], k_ref[energy, s, 1]
            source = times_adjoint(times_wide(high, low, carry), high, low) + source
        carry = source
        b_ref[s] = carry
    v_ref[...] = carry.astype(BF16)


def build_sources(pieces, green, kernels, energy, after):
    slabs, order = green.shape[2:4]
    owners = [k for k in range(len(pieces)) if k >= 2] + [k for k in (1, 0) if k < len(pieces)]
    pieces = [pieces[k] for k in owners]
    return pl.pallas_call(
        ordered(functools.partial(source_body, energy, owners), len(pieces) + 2),
        in_specs=[WHOLE] * (len(pieces) + 2) + [ANYWHERE],
        out_specs=[WHOLE] * 2,
        out_shape=[
            jax.ShapeDtypeStruct((slabs, order, 2 * order), F32),
            jax.ShapeDtypeStruct((order, 2 * order), BF16),
        ],
        scratch_shapes=[pltpu.VMEM((slabs, 2, order, order), BF16)],
        compiler_params=params(),
        cost_estimate=cost(),
        name="sources",
    )(*pieces, green, kernels, after)


def congruence(t_ref, x):
    order = x.shape[0]
    high, low = panels(t_ref)
    if x.dtype == F32:
        inner = times_wide(high, low, x)
    else:
        inner = times_narrow(high, low, x[:, :order], x[:, order:])
    return times_adjoint(inner, high, low)


def entered(refs):
    pair = lax.axis_index("slab") >> 1
    value = jnp.zeros(refs[0].shape, refs[0].dtype)
    for step, ref in enumerate(refs):
        value = jnp.where(pair == step + 1, ref[...], value)
    return value


def pair_body(energy, v_ref, own_ref, sum_ref, t_ref, full_ref, short_ref):
    odd = (lax.axis_index("slab") & 1) == 1
    theirs = v_ref[...]
    x = jnp.where(odd, theirs, own_ref[...])
    base = jnp.where(odd, sum_ref[sum_ref.shape[0] - 1], theirs.astype(F32))
    value = base + congruence(t_ref.at[energy], x)
    full_ref[...] = value
    short_ref[...] = value.astype(BF16)


def pair_sum(arrived, own, sums, maps, energy, after):
    _, order, _ = sums.shape
    return pl.pallas_call(
        ordered(functools.partial(pair_body, energy), 4),
        in_specs=[WHOLE] * 4 + [ANYWHERE],
        out_specs=[WHOLE] * 2,
        out_shape=[jax.ShapeDtypeStruct((order, 2 * order), t) for t in (F32, BF16)],
        compiler_params=params(),
        cost_estimate=cost(),
        name="pair_sum",
    )(arrived, own, sums, maps, after)


def combine(arrived, maps, base, energy, after):
    count = len(arrived)

    def body(*refs):
        t_ref, base_ref, _, out = refs[count:]
        out[...] = (base_ref[...] + congruence(t_ref.at[energy], entered(refs[:count]))).astype(BF16)

    return pl.pallas_call(
        body,
        in_specs=[WHOLE] * (count + 2) + [ANYWHERE],
        out_specs=WHOLE,
        out_shape=jax.ShapeDtypeStruct(base.shape, BF16),
        compiler_params=params(),
        cost_estimate=cost(),
        name="combine",
    )(*arrived, maps, base, after)


def finish_body(energy, arrivals, before_ref, t_ref, m_ref, base_ref, out, blocks, sems):
    slabs, order, _ = base_ref.shape
    odd = (lax.axis_index("slab") & 1) == 1
    before = jnp.where(odd, before_ref[...].astype(F32), 0.0)
    entry = (before + congruence(t_ref.at[energy], entered(arrivals))).astype(BF16)
    maps = m_ref.at[energy]
    rows = maps[...].reshape(slabs * 2 * order, 2 * order)
    both = dot(rows, panel(entry[:, :order], entry[:, order:]))
    copies = []
    for s in range(slabs):
        first = 2 * s * order
        inner = both[first : first + order] + both[first + order : first + 2 * order]
        value = times_adjoint(inner, maps[s, 0], maps[s, 1]) + base_ref[s]
        blocks[s, 0] = value[:, :order]
        blocks[s, 1] = value[:, order:]
        copies.append(pltpu.make_async_copy(blocks.at[s], out.at[:, energy, s], sems.at[s]))
        copies[-1].start()
    for copy in copies:
        copy.wait()


def finish(arrived, before, inner, prefixes, sums, energy, held, after):
    energies, slabs, _, order, _ = prefixes.shape
    operands = list(arrived) + [before, inner, prefixes, sums]
    count = len(operands)
    in_specs = [WHOLE] * count + [ANYWHERE]
    operands.append(after)
    aliases = {}
    if held is not None:
        aliases = {len(operands): 0}
        operands.append(held)
        in_specs.append(ANYWHERE)

    def body(*refs):
        finish_body(energy, refs[: len(arrived)], *refs[len(arrived) : count], *refs[-3:])

    return pl.pallas_call(
        body,
        in_specs=in_specs,
        out_specs=ANYWHERE,
        out_shape=jax.ShapeDtypeStruct((2, energies, slabs, order, order), F32),
        input_output_aliases=aliases,
        scratch_shapes=[pltpu.VMEM((slabs, 2, order, order), F32), pltpu.SemaphoreType.DMA((slabs,))],
        compiler_params=params(),
        cost_estimate=cost(),
        name="finish",
    )(*operands)


def swap(x, k):
    count = lax.axis_size("energy")
    return lax.ppermute(x, "energy", [(i, i ^ k) for i in range(count)])


def other_of_pair(x):
    return lax.ppermute(x, "slab", [(i, i ^ 1) for i in range(lax.axis_size("slab"))])


def forward(x, pair):
    return lax.ppermute(x, "slab", [(2 * pair + i, 2 * pair + 2 + i) for i in range(2)])


def cut(slabs):
    return [(0, slabs - 1), (slabs - 1, 1)] if slabs > 1 else [(0, slabs)]


def per_device(green_lesser, screened_lesser, green_retarded, coupling):
    count = lax.axis_size("energy")
    depth = lax.axis_size("slab")
    if depth % 2 or count & (count - 1):
        raise ValueError("mesh axes")
    _, energies, slabs, order, _ = green_lesser.shape
    far = [k for k in range(count) if k >= 2]
    near = [k for k in range(min(2, count))]
    parts = cut(slabs)

    def first_rows(k, start, size):
        rows = order // count
        begin = (0, 0, start, (lax.axis_index("energy") ^ k) * rows, 0)
        sizes = (2, energies, size, rows, order)
        return [lax.dynamic_slice(x, begin, sizes) for x in (green_lesser, screened_lesser)]

    pieces = [[None] * count for _ in parts]
    for chunk, (start, size) in enumerate(parts):
        for k in far + near:
            block = jnp.stack(first_rows(k, start, size))
            pieces[chunk][k] = swap(block, k) if k else block
    token = pieces[0][0]

    kernels, prefixes = build_maps(green_retarded, coupling, token)
    token = kernels
    mine = [prefixes[e, slabs - 1] for e in range(energies)]
    other = [other_of_pair(x) for x in mine]

    blocks = ()
    for chunk, (start, size) in enumerate(parts):
        if chunk == len(parts) - 1:
            pair_step, plane, inner = pair_maps(mine, other, energies, token)
            token = plane
        blocks = convolve(pieces[chunk], start, slabs, size, blocks, token)
        token = blocks[0]
    sigma = [[None] * count for _ in range(energies)]
    for e in range(energies):
        for k in range(count):
            block = blocks[k * energies + e]
            sigma[e][k] = swap(block, k) if k else block

    pairs = depth // 2
    sums, own, ours = ([None] * energies for _ in range(3))
    running, carry = [None] * energies, [None] * energies
    arrived = [[] for _ in range(energies)]

    def stage(e, step):
        nonlocal token
        if step == 0:
            sums[e], own[e] = build_sources(sigma[e], green_retarded, kernels, e, token)
            token = own[e]
            ours[e] = other_of_pair(own[e])
        elif step == 1:
            running[e], carry[e] = pair_sum(ours[e], own[e], sums[e], pair_step, e, token)
            token = carry[e]
            arrived[e].append(forward(carry[e], 0))
        else:
            carry[e] = token = combine(arrived[e], plane, running[e], e, token)
            arrived[e].append(forward(carry[e], step - 1))

    last = max(pairs - 1, 1)
    for step in range(last + 1):
        for e in range(energies):
            stage(e, step)
    result = None
    for e in range(energies):
        result = finish(arrived[e], ours[e], inner, prefixes, sums[e], e, result, token)
    return result


def solution(mesh):
    placed = (
        P(None, "energy", "slab", None, None),
        P(None, "energy", "slab", None, None),
        P(None, "energy", "slab", None, None),
        P(None, "slab", None, None),
    )
    return jax.shard_map(
        per_device,
        mesh=mesh,
        in_specs=placed,
        out_specs=P(None, "energy", "slab", None, None),
        check_vma=False,
    )
```

```python
import functools

import jax
import jax.numpy as jnp
from jax import lax
from jax.experimental import pallas as pl
from jax.experimental.pallas import tpu as pltpu
from jax.sharding import PartitionSpec as P

BF16 = jnp.bfloat16
F32 = jnp.float32
VMEM_LIMIT = 24 * 1024 * 1024


def params():
    return pltpu.CompilerParams(vmem_limit_bytes=VMEM_LIMIT)


def ordered(body, count, extra=1):
    def run(*refs):
        body(*refs[:count], *refs[count + extra :])

    return run


ANYWHERE = pl.BlockSpec(memory_space=pl.ANY)
WHOLE = pl.BlockSpec(memory_space=pltpu.VMEM)


def cost():
    return pl.CostEstimate(flops=0, bytes_accessed=0, transcendentals=0)


def split(value):
    high = value.astype(BF16)
    low = (value - high.astype(F32)).astype(BF16)
    return high, low


def panel(re, im):
    return jnp.concatenate(
        [jnp.concatenate([re, im], axis=1), jnp.concatenate([-im, re], axis=1)], axis=0
    )


def dot(left, right):
    return lax.dot_general(left, right, (((1,), (0,)), ((), ())), preferred_element_type=F32)


def dot_nt(left, right):
    return lax.dot_general(left, right, (((1,), (1,)), ((), ())), preferred_element_type=F32)


def times_wide(a_high, a_low, x):
    order = x.shape[0]
    x_high, x_low = split(x)
    xh = panel(x_high[:, :order], x_high[:, order:])
    xl = panel(x_low[:, :order], x_low[:, order:])
    left = jnp.concatenate([a_high, a_high, a_low], axis=1)
    return dot(left, jnp.concatenate([xh, xl, xh], axis=0))


def times_narrow(a_high, a_low, re, im):
    xp = panel(re, im)
    left = jnp.concatenate([a_high, a_low], axis=1)
    return dot(left, jnp.concatenate([xp, xp], axis=0))


def times_adjoint(y, t_high, t_low):
    order = y.shape[0]
    y_high, y_low = split(y)
    th = panel(t_high[:, :order], t_high[:, order:])
    tl = panel(t_low[:, :order], t_low[:, order:])
    left = jnp.concatenate([y_high, y_low, y_high], axis=1)
    return dot_nt(left, jnp.concatenate([th, th, tl], axis=1))


def panels(ref):
    return ref[0], ref[1]


def store_map(ref, value):
    high, low = split(value)
    ref[0] = high
    ref[1] = low


def pack_body(wanted, *refs):
    sources, outs, sems = refs[:2], refs[-1 - len(wanted) : -1], refs[-1]
    copies = []
    for out, (k, start) in zip(outs, wanted):
        size, rows = out.shape[3:5]
        begin = pl.multiple_of((lax.axis_index("energy") ^ k) * rows, rows)
        for part in range(2):
            block = sources[part].at[:, :, pl.ds(start, size), pl.ds(begin, rows), :]
            copies.append(pltpu.make_async_copy(block, out.at[part], sems.at[len(copies)]))
    for copy in copies:
        copy.start()
    for copy in copies:
        copy.wait()


def pack(green, screen, wanted, count, after):
    _, energies, _, order, _ = green.shape
    return pl.pallas_call(
        functools.partial(pack_body, [w[:2] for w in wanted]),
        in_specs=[ANYWHERE] * 3,
        out_specs=[WHOLE] * len(wanted),
        out_shape=[
            jax.ShapeDtypeStruct((2, 2, energies, size, order // count, order), BF16) for _, _, size in wanted
        ],
        scratch_shapes=[pltpu.SemaphoreType.DMA((2 * len(wanted),))],
        compiler_params=params(),
        cost_estimate=cost(),
        name="pack",
    )(green, screen, after)


def maps_body(g_ref, c_ref, k_ref, p_ref, carry):
    left = jnp.concatenate([g_ref[0], g_ref[1]], axis=1)
    value = dot(left, panel(c_ref[0], c_ref[1]))
    store_map(k_ref, value)

    @pl.when(pl.program_id(1) == 0)
    def _():
        carry[...] = value

    @pl.when(pl.program_id(1) > 0)
    def _():
        high, low = panels(k_ref)
        carry[...] = times_wide(high, low, carry[...])

    store_map(p_ref, carry[...])


def build_maps(green, coupling, *after):
    _, energies, slabs, order, _ = green.shape
    shape = jax.ShapeDtypeStruct((energies, slabs, 2, order, 2 * order), BF16)
    out_spec = pl.BlockSpec((None, None, 2, order, 2 * order), lambda e, s: (e, s, 0, 0, 0))
    return pl.pallas_call(
        lambda *refs: maps_body(*refs[:2], *refs[2 + len(after) :]),
        grid=(energies, slabs),
        in_specs=[
            pl.BlockSpec((2, None, None, order, order), lambda e, s: (0, e, s, 0, 0)),
            pl.BlockSpec((2, None, order, order), lambda e, s: (0, s, 0, 0)),
        ]
        + [ANYWHERE] * len(after),
        out_specs=[out_spec, out_spec],
        out_shape=[shape, shape],
        scratch_shapes=[pltpu.VMEM((order, 2 * order), F32)],
        compiler_params=params(),
        cost_estimate=cost(),
        name="maps",
    )(green, coupling, *after)


def one_map(maps, energy):
    if isinstance(maps, list):
        return maps[energy], pl.BlockSpec(maps[energy].shape, lambda *_: (0, 0, 0))
    return maps, pl.BlockSpec((None,) + maps.shape[1:], lambda *_: (energy, 0, 0, 0))


def pair_maps_body(energies, *refs):
    step, plane, inner = refs[-3:]
    odd = (lax.axis_index("slab") & 1) == 1
    for e in range(energies):
        mine, other = refs[2 * e], refs[2 * e + 1]
        order = mine.shape[1]
        first = [jnp.where(odd, mine[part], other[part]) for part in range(2)]
        second = [jnp.where(odd, other[part], mine[part]).astype(F32) for part in range(2)]
        store_map(plane.at[e], times_wide(*first, second[0] + second[1]))
        row = lax.broadcasted_iota(jnp.int32, (order, 2 * order), 0)
        column = lax.broadcasted_iota(jnp.int32, (order, 2 * order), 1)
        unit = jnp.where(row == column, 1.0, 0.0)
        for part in range(2):
            step[e, part] = first[part]
            identity = unit if part == 0 else jnp.zeros_like(unit)
            inner[e, part] = jnp.where(odd, other[part].astype(F32), identity).astype(BF16)


def pair_maps(mine, other, energies, after):
    pairs = [one_map(maps, e) for e in range(energies) for maps in (mine, other)]
    shape = (energies,) + pairs[0][1].block_shape[-3:]
    return pl.pallas_call(
        ordered(functools.partial(pair_maps_body, energies), 2 * energies),
        grid=(1,),
        in_specs=[spec for _, spec in pairs] + [ANYWHERE],
        out_specs=[pl.BlockSpec(shape, lambda i: (0, 0, 0, 0))] * 3,
        out_shape=[jax.ShapeDtypeStruct(shape, BF16)] * 3,
        compiler_params=params(),
        cost_estimate=cost(),
        name="pair_maps",
    )(*[maps for maps, _ in pairs], after)


def convolve_body(pairs, energies, shared, *refs):
    count = len(pairs)
    taken = sum(1 + pair for pair in pairs)
    ins, outs = list(refs[:taken]), refs[taken + 1 + shared :]
    green, screen, total = refs[-3:]
    me = lax.axis_index("energy")
    points = count * energies
    middle = points // 2
    rows, columns = green.shape[2:]
    for k in range(count):
        base = (me ^ k) * energies
        piece = ins.pop(0)
        halves = (piece, ins.pop(0)) if pairs[k] else (piece.at[0], piece.at[1])
        for e in range(energies):
            green[:, base + e] = halves[0][:, e].astype(F32)
            screen[:, base + e] = halves[1][:, e].astype(F32)

    def tile(index, _):
        row = pl.multiple_of(index * 8, 8)
        for col in range(0, columns, 128):
            at = (pl.ds(row, 8), pl.ds(col, 128))
            gr = [green[(0, m) + at] for m in range(points)]
            gi = [green[(1, m) + at] for m in range(points)]
            wr = [screen[(0, m) + at] for m in range(points)]
            wi = [screen[(1, m) + at] for m in range(points)]
            for n in range(points):
                re = None
                im = None
                for m in range(points):
                    lag = n - m + middle
                    if 0 <= lag < points:
                        a = gr[m] * wr[lag] - gi[m] * wi[lag]
                        b = gr[m] * wi[lag] + gi[m] * wr[lag]
                        re = a if re is None else re + a
                        im = b if im is None else im + b
                total[(n, 0) + at] = -im / points
                total[(n, 1) + at] = re / points
        return 0

    lax.fori_loop(0, rows // 8, tile, 0)
    for k in range(count):
        base = (me ^ k) * energies
        for e in range(energies):
            outs[k * energies + e][...] = total[base + e].astype(BF16)


def convolve(pieces, start, slabs, size, held, after):
    count = len(pieces)
    pairs = [isinstance(piece, tuple) for piece in pieces]
    operands, in_specs = [], []
    for piece, pair in zip(pieces, pairs):
        if pair:
            operands += piece
            energies, _, rows, columns = piece[0].shape[1:]
            in_specs += [pl.BlockSpec((2, energies, None, rows, columns), lambda s: (0, 0, s + start, 0, 0))] * 2
        else:
            operands.append(piece)
            energies, _, rows, columns = piece.shape[2:]
            first = start if piece.shape[3] == slabs else 0
            block = (2, 2, energies, None, rows, columns)
            in_specs.append(pl.BlockSpec(block, lambda s, first=first: (0, 0, 0, s + first, 0, 0)))
    points = count * energies
    whole = pl.BlockSpec((None, 2, rows, columns), lambda s: (s + start, 0, 0, 0))
    outs = pl.pallas_call(
        functools.partial(convolve_body, pairs, energies, len(held)),
        grid=(size,),
        in_specs=in_specs + [ANYWHERE] * (1 + len(held)),
        out_specs=[whole] * points,
        out_shape=[jax.ShapeDtypeStruct((slabs, 2, rows, columns), BF16)] * points,
        input_output_aliases={len(operands) + 1 + i: i for i in range(len(held))},
        scratch_shapes=[
            pltpu.VMEM((2, points, rows, columns), F32),
            pltpu.VMEM((2, points, rows, columns), F32),
            pltpu.VMEM((points, 2, rows, columns), F32),
        ],
        compiler_params=params(),
        cost_estimate=cost(),
        name="convolve",
    )(*operands, after, *held)
    return outs


def source_body(energy, owners, *refs):
    pieces = refs[: len(owners)]
    g_ref, k_ref, b_ref, v_ref, sigma = refs[len(owners) :]
    me = lax.axis_index("energy")
    for piece, k in zip(pieces, owners):
        slabs, _, rows, _ = piece.shape
        start = pl.multiple_of((me ^ k) * rows, rows)
        for s in range(slabs):
            for part in range(2):
                sigma[s, part, pl.ds(start, rows), :] = piece[s, part]

    carry = None
    for s in range(sigma.shape[0]):
        green_re, green_im = g_ref[0, energy, s], g_ref[1, energy, s]
        left = jnp.concatenate([green_re, green_im], axis=1)
        mixed = dot(left, panel(sigma[s, 0], sigma[s, 1])).astype(BF16)
        source = dot_nt(mixed, panel(green_re, green_im))
        if carry is not None:
            high, low = k_ref[energy, s, 0], k_ref[energy, s, 1]
            source = times_adjoint(times_wide(high, low, carry), high, low) + source
        carry = source
        b_ref[s] = carry
    v_ref[...] = carry.astype(BF16)


def build_sources(pieces, green, kernels, energy, after):
    slabs, order = green.shape[2:4]
    owners = [k for k in range(len(pieces)) if k >= 2] + [k for k in (1, 0) if k < len(pieces)]
    pieces = [pieces[k] for k in owners]
    return pl.pallas_call(
        ordered(functools.partial(source_body, energy, owners), len(pieces) + 2),
        in_specs=[WHOLE] * (len(pieces) + 2) + [ANYWHERE],
        out_specs=[WHOLE] * 2,
        out_shape=[
            jax.ShapeDtypeStruct((slabs, order, 2 * order), F32),
            jax.ShapeDtypeStruct((order, 2 * order), BF16),
        ],
        scratch_shapes=[pltpu.VMEM((slabs, 2, order, order), BF16)],
        compiler_params=params(),
        cost_estimate=cost(),
        name="sources",
    )(*pieces, green, kernels, after)


def congruence(t_ref, x):
    order = x.shape[0]
    high, low = panels(t_ref)
    if x.dtype == F32:
        inner = times_wide(high, low, x)
    else:
        inner = times_narrow(high, low, x[:, :order], x[:, order:])
    return times_adjoint(inner, high, low)


def entered(refs):
    pair = lax.axis_index("slab") >> 1
    value = jnp.zeros(refs[0].shape, refs[0].dtype)
    for step, ref in enumerate(refs):
        value = jnp.where(pair == step + 1, ref[...], value)
    return value


def pair_body(energy, v_ref, own_ref, sum_ref, t_ref, full_ref, short_ref):
    odd = (lax.axis_index("slab") & 1) == 1
    theirs = v_ref[...]
    x = jnp.where(odd, theirs, own_ref[...])
    base = jnp.where(odd, sum_ref[sum_ref.shape[0] - 1], theirs.astype(F32))
    value = base + congruence(t_ref.at[energy], x)
    full_ref[...] = value
    short_ref[...] = value.astype(BF16)


def pair_sum(arrived, own, sums, maps, energy, after):
    _, order, _ = sums.shape
    return pl.pallas_call(
        ordered(functools.partial(pair_body, energy), 4),
        in_specs=[WHOLE] * 4 + [ANYWHERE],
        out_specs=[WHOLE] * 2,
        out_shape=[jax.ShapeDtypeStruct((order, 2 * order), t) for t in (F32, BF16)],
        compiler_params=params(),
        cost_estimate=cost(),
        name="pair_sum",
    )(arrived, own, sums, maps, after)


def combine(arrived, maps, base, energy, after):
    count = len(arrived)

    def body(*refs):
        t_ref, base_ref, _, out = refs[count:]
        out[...] = (base_ref[...] + congruence(t_ref.at[energy], entered(refs[:count]))).astype(BF16)

    return pl.pallas_call(
        body,
        in_specs=[WHOLE] * (count + 2) + [ANYWHERE],
        out_specs=WHOLE,
        out_shape=jax.ShapeDtypeStruct(base.shape, BF16),
        compiler_params=params(),
        cost_estimate=cost(),
        name="combine",
    )(*arrived, maps, base, after)


def spread(maps, entry, sums, store):
    slabs, order, _ = sums.shape
    rows = maps[...].reshape(slabs * 2 * order, 2 * order)
    both = dot(rows, panel(entry[:, :order], entry[:, order:]))
    for s in range(slabs):
        first = 2 * s * order
        inner = both[first : first + order] + both[first + order : first + 2 * order]
        store(s, times_adjoint(inner, maps[s, 0], maps[s, 1]) + sums[s])


def from_partner(before_ref):
    odd = (lax.axis_index("slab") & 1) == 1
    return jnp.where(odd, before_ref[...], jnp.zeros_like(before_ref))


def entry_maps(prefixes, inner, energy, after):
    _, slabs, _, order, _ = prefixes.shape

    def body(p_ref, i_ref, _, out):
        high, low = panels(i_ref.at[energy])
        ih = panel(high[:, :order], high[:, order:])
        il = panel(low[:, :order], low[:, order:])
        for s in range(slabs):
            both = dot(p_ref[energy, s].reshape(2 * order, 2 * order), ih)
            store_map(out.at[0, s], both[:order] + both[order:] + dot(p_ref[energy, s, 0], il))

    return pl.pallas_call(
        body,
        in_specs=[WHOLE] * 2 + [ANYWHERE],
        out_specs=WHOLE,
        out_shape=jax.ShapeDtypeStruct((1,) + prefixes.shape[1:], BF16),
        compiler_params=params(),
        cost_estimate=cost(),
        name="entry_maps",
    )(prefixes, inner, after)


def part_known(before, prefixes, sums, energy, after):
    def body(before_ref, p_ref, sum_ref, _, out):
        def store(s, value):
            out[s] = value

        spread(p_ref.at[energy], from_partner(before_ref), sum_ref, store)

    return pl.pallas_call(
        body,
        in_specs=[WHOLE] * 3 + [ANYWHERE],
        out_specs=WHOLE,
        out_shape=jax.ShapeDtypeStruct(sums.shape, F32),
        compiler_params=params(),
        cost_estimate=cost(),
        name="part_known",
    )(before, prefixes, sums, after)


def finish_body(energy, maps_index, arrivals, before, m_ref, base_ref, out, blocks, sems):
    order = base_ref.shape[1]
    entry = entered(arrivals)
    if before is not None:
        before_ref, t_ref = before
        whole = from_partner(before_ref).astype(F32) + congruence(t_ref.at[energy], entry)
        entry = whole.astype(BF16)
    copies = []

    def store(s, value):
        blocks[s, 0] = value[:, :order]
        blocks[s, 1] = value[:, order:]
        copies.append(pltpu.make_async_copy(blocks.at[s], out.at[:, energy, s], sems.at[s]))
        copies[-1].start()

    spread(m_ref.at[maps_index], entry, base_ref, store)
    for copy in copies:
        copy.wait()


def finish(arrived, before, maps, maps_index, sums, energy, energies, held, after):
    slabs, order, _ = sums.shape
    count = len(arrived)
    extra = [] if before is None else list(before)
    operands = list(arrived) + extra + [maps, sums]
    in_specs = [WHOLE] * len(operands) + [ANYWHERE]
    operands.append(after)
    aliases = {}
    if held is not None:
        aliases = {len(operands): 0}
        operands.append(held)
        in_specs.append(ANYWHERE)

    def body(*refs):
        second = count + len(extra)
        finish_body(
            energy,
            maps_index,
            refs[:count],
            refs[count:second] if extra else None,
            *refs[second : second + 2],
            *refs[-3:],
        )

    return pl.pallas_call(
        body,
        in_specs=in_specs,
        out_specs=ANYWHERE,
        out_shape=jax.ShapeDtypeStruct((2, energies, slabs, order, order), F32),
        input_output_aliases=aliases,
        scratch_shapes=[pltpu.VMEM((slabs, 2, order, order), F32), pltpu.SemaphoreType.DMA((slabs,))],
        compiler_params=params(),
        cost_estimate=cost(),
        name="finish",
    )(*operands)


def swap(x, k):
    count = lax.axis_size("energy")
    return lax.ppermute(x, "energy", [(i, i ^ k) for i in range(count)])


def other_of_pair(x):
    return lax.ppermute(x, "slab", [(i, i ^ 1) for i in range(lax.axis_size("slab"))])


def forward(x, pair):
    return lax.ppermute(x, "slab", [(2 * pair + i, 2 * pair + 2 + i) for i in range(2)])


def cut(slabs):
    return [(0, slabs - 1), (slabs - 1, 1)] if slabs > 1 else [(0, slabs)]


def per_device(green_lesser, screened_lesser, green_retarded, coupling):
    count = lax.axis_size("energy")
    depth = lax.axis_size("slab")
    if depth % 2 or count & (count - 1):
        raise ValueError("mesh axes")
    _, energies, slabs, order, _ = green_lesser.shape
    far = [k for k in range(count) if k >= 2]
    near = [k for k in range(min(2, count))]
    parts = cut(slabs)

    def first_rows(k, start, size):
        rows = order // count
        begin = (0, 0, start, (lax.axis_index("energy") ^ k) * rows, 0)
        sizes = (2, energies, size, rows, order)
        return [lax.dynamic_slice(x, begin, sizes) for x in (green_lesser, screened_lesser)]

    pieces = [[None] * count for _ in parts]
    places = [(chunk, k) for chunk in range(len(parts)) for k in far + near]
    chunk, k = places[0]
    token = jnp.stack(first_rows(k, *parts[chunk]))
    pieces[chunk][k] = swap(token, k) if k else token
    urgent = [place for place in places[1:] if place[0] == 0 and place[1]]
    for group in (urgent, [place for place in places[1:] if place not in urgent]):
        if group:
            packed = pack(green_lesser, screened_lesser, [(k,) + parts[chunk] for chunk, k in group], count, token)
            for (chunk, k), block in zip(group, packed):
                pieces[chunk][k] = swap(block, k) if k else block
            token = packed[0]

    kernels, prefixes = build_maps(green_retarded, coupling, token)
    token = kernels
    mine = [prefixes[e, slabs - 1] for e in range(energies)]
    other = [other_of_pair(x) for x in mine]

    blocks = ()
    for chunk, (start, size) in enumerate(parts):
        if chunk == len(parts) - 1:
            pair_step, plane, inner = pair_maps(mine, other, energies, token)
            token = plane
        blocks = convolve(pieces[chunk], start, slabs, size, blocks, token)
        token = blocks[0]
    sigma = [[None] * count for _ in range(energies)]
    for e in range(energies):
        for k in range(count):
            block = blocks[k * energies + e]
            sigma[e][k] = swap(block, k) if k else block

    pairs = depth // 2
    final = energies - 1
    entries = token = entry_maps(prefixes, inner, final, token)
    known = None
    sums, own, ours = ([None] * energies for _ in range(3))
    running, carry = [None] * energies, [None] * energies
    arrived = [[] for _ in range(energies)]

    def stage(e, step):
        nonlocal token
        if step == 0:
            sums[e], own[e] = build_sources(sigma[e], green_retarded, kernels, e, token)
            token = own[e]
            ours[e] = other_of_pair(own[e])
        elif step == 1:
            running[e], carry[e] = pair_sum(ours[e], own[e], sums[e], pair_step, e, token)
            token = carry[e]
            arrived[e].append(forward(carry[e], 0))
        else:
            carry[e] = token = combine(arrived[e], plane, running[e], e, token)
            arrived[e].append(forward(carry[e], step - 1))

    last = max(pairs - 1, 1)
    for step in range(last + 1):
        for e in range(energies):
            stage(e, step)
        if step == min(2, last):
            known = token = part_known(ours[final], prefixes, sums[final], final, token)
    result = None
    for e in range(final):
        result = finish(
            arrived[e], (ours[e], inner), prefixes, e, sums[e], e, energies, result, token
        )
    return finish(arrived[final], None, entries, 0, known, final, energies, result, token)


def solution(mesh):
    placed = (
        P(None, "energy", "slab", None, None),
        P(None, "energy", "slab", None, None),
        P(None, "energy", "slab", None, None),
        P(None, "slab", None, None),
    )
    return jax.shard_map(
        per_device,
        mesh=mesh,
        in_specs=placed,
        out_specs=P(None, "energy", "slab", None, None),
        check_vma=False,
    )
```

```python
import functools

import jax
import jax.numpy as jnp
from jax import lax
from jax.experimental import pallas as pl
from jax.experimental.pallas import tpu as pltpu
from jax.sharding import PartitionSpec as P

BF16 = jnp.bfloat16
F32 = jnp.float32
VMEM_LIMIT = 36 * 1024 * 1024


def params():
    return pltpu.CompilerParams(vmem_limit_bytes=VMEM_LIMIT)


def ordered(body, count, extra=1):
    def run(*refs):
        body(*refs[:count], *refs[count + extra :])

    return run


ANYWHERE = pl.BlockSpec(memory_space=pl.ANY)
WHOLE = pl.BlockSpec(memory_space=pltpu.VMEM)


def cost():
    return pl.CostEstimate(flops=0, bytes_accessed=0, transcendentals=0)


def split(value):
    high = value.astype(BF16)
    low = (value - high.astype(F32)).astype(BF16)
    return high, low


def panel(re, im):
    return jnp.concatenate(
        [jnp.concatenate([re, im], axis=1), jnp.concatenate([-im, re], axis=1)], axis=0
    )


def dot(left, right):
    return lax.dot_general(left, right, (((1,), (0,)), ((), ())), preferred_element_type=F32)


def dot_nt(left, right):
    return lax.dot_general(left, right, (((1,), (1,)), ((), ())), preferred_element_type=F32)


def times_wide(a_high, a_low, x):
    order = x.shape[0]
    x_high, x_low = split(x)
    both = dot(jnp.concatenate([a_high, a_low], axis=0), panel(x_high[:, :order], x_high[:, order:]))
    return both[:order] + both[order:] + dot(a_high, panel(x_low[:, :order], x_low[:, order:]))


def times_narrow(a_high, a_low, re, im):
    order = re.shape[0]
    both = dot(jnp.concatenate([a_high, a_low], axis=0), panel(re, im))
    return both[:order] + both[order:]


def times_adjoint(y, t_high, t_low):
    order = y.shape[0]
    y_high, y_low = split(y)
    th = panel(t_high[:, :order], t_high[:, order:])
    tl = panel(t_low[:, :order], t_low[:, order:])
    both = dot_nt(jnp.concatenate([y_high, y_low], axis=0), th)
    return both[:order] + both[order:] + dot_nt(y_high, tl)


def panels(ref):
    return ref[0], ref[1]


def store_map(ref, value):
    high, low = split(value)
    ref[0] = high
    ref[1] = low


def pack_body(wanted, *refs):
    sources, outs, sems = refs[:2], refs[-1 - len(wanted) : -1], refs[-1]
    copies = []
    for out, (k, start) in zip(outs, wanted):
        size, rows = out.shape[3:5]
        begin = pl.multiple_of((lax.axis_index("energy") ^ k) * rows, rows)
        for part in range(2):
            block = sources[part].at[:, :, pl.ds(start, size), pl.ds(begin, rows), :]
            copies.append(pltpu.make_async_copy(block, out.at[part], sems.at[len(copies)]))
    for copy in copies:
        copy.start()
    for copy in copies:
        copy.wait()


def pack(green, screen, wanted, count, after):
    _, energies, _, order, _ = green.shape
    return pl.pallas_call(
        functools.partial(pack_body, [w[:2] for w in wanted]),
        in_specs=[ANYWHERE] * 3,
        out_specs=[WHOLE] * len(wanted),
        out_shape=[
            jax.ShapeDtypeStruct((2, 2, energies, size, order // count, order), BF16) for _, _, size in wanted
        ],
        scratch_shapes=[pltpu.SemaphoreType.DMA((2 * len(wanted),))],
        compiler_params=params(),
        cost_estimate=cost(),
        name="pack",
    )(green, screen, after)


def maps_body(g_ref, c_ref, k_ref, p_ref, carry):
    left = jnp.concatenate([g_ref[0], g_ref[1]], axis=1)
    value = dot(left, panel(c_ref[0], c_ref[1]))
    store_map(k_ref, value)

    @pl.when(pl.program_id(1) == 0)
    def _():
        carry[...] = value

    @pl.when(pl.program_id(1) > 0)
    def _():
        high, low = panels(k_ref)
        carry[...] = times_wide(high, low, carry[...])

    store_map(p_ref, carry[...])


def build_maps(green, coupling, *after):
    _, energies, slabs, order, _ = green.shape
    shape = jax.ShapeDtypeStruct((energies, slabs, 2, order, 2 * order), BF16)
    out_spec = pl.BlockSpec((None, None, 2, order, 2 * order), lambda e, s: (e, s, 0, 0, 0))
    return pl.pallas_call(
        lambda *refs: maps_body(*refs[:2], *refs[2 + len(after) :]),
        grid=(energies, slabs),
        in_specs=[
            pl.BlockSpec((2, None, None, order, order), lambda e, s: (0, e, s, 0, 0)),
            pl.BlockSpec((2, None, order, order), lambda e, s: (0, s, 0, 0)),
        ]
        + [ANYWHERE] * len(after),
        out_specs=[out_spec, out_spec],
        out_shape=[shape, shape],
        scratch_shapes=[pltpu.VMEM((order, 2 * order), F32)],
        compiler_params=params(),
        cost_estimate=cost(),
        name="maps",
    )(green, coupling, *after)


def one_map(maps, energy):
    if isinstance(maps, list):
        return maps[energy], pl.BlockSpec(maps[energy].shape, lambda *_: (0, 0, 0))
    return maps, pl.BlockSpec((None,) + maps.shape[1:], lambda *_: (energy, 0, 0, 0))


def pair_maps_body(energies, *refs):
    step, plane, inner = refs[-3:]
    odd = (lax.axis_index("slab") & 1) == 1
    for e in range(energies):
        mine, other = refs[2 * e], refs[2 * e + 1]
        order = mine.shape[1]
        first = [jnp.where(odd, mine[part], other[part]) for part in range(2)]
        second = [jnp.where(odd, other[part], mine[part]).astype(F32) for part in range(2)]
        store_map(plane.at[e], times_wide(*first, second[0] + second[1]))
        row = lax.broadcasted_iota(jnp.int32, (order, 2 * order), 0)
        column = lax.broadcasted_iota(jnp.int32, (order, 2 * order), 1)
        unit = jnp.where(row == column, 1.0, 0.0)
        for part in range(2):
            step[e, part] = first[part]
            identity = unit if part == 0 else jnp.zeros_like(unit)
            inner[e, part] = jnp.where(odd, other[part].astype(F32), identity).astype(BF16)


def pair_maps(mine, other, energies, after):
    pairs = [one_map(maps, e) for e in range(energies) for maps in (mine, other)]
    shape = (energies,) + pairs[0][1].block_shape[-3:]
    return pl.pallas_call(
        ordered(functools.partial(pair_maps_body, energies), 2 * energies),
        grid=(1,),
        in_specs=[spec for _, spec in pairs] + [ANYWHERE],
        out_specs=[pl.BlockSpec(shape, lambda i: (0, 0, 0, 0))] * 3,
        out_shape=[jax.ShapeDtypeStruct(shape, BF16)] * 3,
        compiler_params=params(),
        cost_estimate=cost(),
        name="pair_maps",
    )(*[maps for maps, _ in pairs], after)


def convolve_body(pairs, energies, shared, *refs):
    count = len(pairs)
    taken = sum(1 + pair for pair in pairs)
    ins, outs = list(refs[:taken]), refs[taken + 1 + shared :]
    green, screen, total = refs[-3:]
    me = lax.axis_index("energy")
    points = count * energies
    middle = points // 2
    rows, columns = green.shape[2:]
    for k in range(count):
        base = (me ^ k) * energies
        piece = ins.pop(0)
        halves = (piece, ins.pop(0)) if pairs[k] else (piece.at[0], piece.at[1])
        for e in range(energies):
            green[:, base + e] = halves[0][:, e].astype(F32)
            screen[:, base + e] = halves[1][:, e].astype(F32)

    def tile(index, _):
        row = pl.multiple_of(index * 8, 8)
        for col in range(0, columns, 128):
            at = (pl.ds(row, 8), pl.ds(col, 128))
            gr = [green[(0, m) + at] for m in range(points)]
            gi = [green[(1, m) + at] for m in range(points)]
            wr = [screen[(0, m) + at] for m in range(points)]
            wi = [screen[(1, m) + at] for m in range(points)]
            for n in range(points):
                re = None
                im = None
                for m in range(points):
                    lag = n - m + middle
                    if 0 <= lag < points:
                        a = gr[m] * wr[lag] - gi[m] * wi[lag]
                        b = gr[m] * wi[lag] + gi[m] * wr[lag]
                        re = a if re is None else re + a
                        im = b if im is None else im + b
                total[(n, 0) + at] = -im / points
                total[(n, 1) + at] = re / points
        return 0

    lax.fori_loop(0, rows // 8, tile, 0)
    for k in range(count):
        base = (me ^ k) * energies
        for e in range(energies):
            outs[k * energies + e][...] = total[base + e].astype(BF16)


def convolve(pieces, start, slabs, size, held, after):
    count = len(pieces)
    pairs = [isinstance(piece, tuple) for piece in pieces]
    operands, in_specs = [], []
    for piece, pair in zip(pieces, pairs):
        if pair:
            operands += piece
            energies, _, rows, columns = piece[0].shape[1:]
            in_specs += [pl.BlockSpec((2, energies, None, rows, columns), lambda s: (0, 0, s + start, 0, 0))] * 2
        else:
            operands.append(piece)
            energies, _, rows, columns = piece.shape[2:]
            first = start if piece.shape[3] == slabs else 0
            block = (2, 2, energies, None, rows, columns)
            in_specs.append(pl.BlockSpec(block, lambda s, first=first: (0, 0, 0, s + first, 0, 0)))
    points = count * energies
    whole = pl.BlockSpec((None, 2, rows, columns), lambda s: (s + start, 0, 0, 0))
    outs = pl.pallas_call(
        functools.partial(convolve_body, pairs, energies, len(held)),
        grid=(size,),
        in_specs=in_specs + [ANYWHERE] * (1 + len(held)),
        out_specs=[whole] * points,
        out_shape=[jax.ShapeDtypeStruct((slabs, 2, rows, columns), BF16)] * points,
        input_output_aliases={len(operands) + 1 + i: i for i in range(len(held))},
        scratch_shapes=[
            pltpu.VMEM((2, points, rows, columns), F32),
            pltpu.VMEM((2, points, rows, columns), F32),
            pltpu.VMEM((points, 2, rows, columns), F32),
        ],
        compiler_params=params(),
        cost_estimate=cost(),
        name="convolve",
    )(*operands, after, *held)
    return outs


def source_body(energy, owners, *refs):
    pieces = refs[: len(owners)]
    g_ref, k_ref, b_ref, v_ref, sigma = refs[len(owners) :]
    me = lax.axis_index("energy")
    for piece, k in zip(pieces, owners):
        slabs, _, rows, _ = piece.shape
        start = pl.multiple_of((me ^ k) * rows, rows)
        for s in range(slabs):
            for part in range(2):
                sigma[s, part, pl.ds(start, rows), :] = piece[s, part]

    carry = None
    for s in range(sigma.shape[0]):
        green_re, green_im = g_ref[0, energy, s], g_ref[1, energy, s]
        left = jnp.concatenate([green_re, green_im], axis=1)
        mixed = dot(left, panel(sigma[s, 0], sigma[s, 1])).astype(BF16)
        source = dot_nt(mixed, panel(green_re, green_im))
        if carry is not None:
            high, low = k_ref[energy, s, 0], k_ref[energy, s, 1]
            source = times_adjoint(times_wide(high, low, carry), high, low) + source
        carry = source
        b_ref[s] = carry
    v_ref[...] = carry.astype(BF16)


def build_sources(pieces, green, kernels, energy, after):
    slabs, order = green.shape[2:4]
    owners = [k for k in range(len(pieces)) if k >= 2] + [k for k in (1, 0) if k < len(pieces)]
    pieces = [pieces[k] for k in owners]
    return pl.pallas_call(
        ordered(functools.partial(source_body, energy, owners), len(pieces) + 2),
        in_specs=[WHOLE] * (len(pieces) + 2) + [ANYWHERE],
        out_specs=[WHOLE] * 2,
        out_shape=[
            jax.ShapeDtypeStruct((slabs, order, 2 * order), F32),
            jax.ShapeDtypeStruct((order, 2 * order), BF16),
        ],
        scratch_shapes=[pltpu.VMEM((slabs, 2, order, order), BF16)],
        compiler_params=params(),
        cost_estimate=cost(),
        name="sources",
    )(*pieces, green, kernels, after)


def congruence(t_ref, x):
    order = x.shape[0]
    high, low = panels(t_ref)
    if x.dtype == F32:
        inner = times_wide(high, low, x)
    else:
        inner = times_narrow(high, low, x[:, :order], x[:, order:])
    return times_adjoint(inner, high, low)


def entered(refs):
    pair = lax.axis_index("slab") >> 1
    value = jnp.zeros(refs[0].shape, refs[0].dtype)
    for step, ref in enumerate(refs):
        value = jnp.where(pair == step + 1, ref[...], value)
    return value


def pair_body(energy, v_ref, own_ref, sum_ref, t_ref, full_ref, short_ref):
    odd = (lax.axis_index("slab") & 1) == 1
    theirs = v_ref[...]
    x = jnp.where(odd, theirs, own_ref[...])
    base = jnp.where(odd, sum_ref[sum_ref.shape[0] - 1], theirs.astype(F32))
    value = base + congruence(t_ref.at[energy], x)
    full_ref[...] = value
    short_ref[...] = value.astype(BF16)


def pair_sum(arrived, own, sums, maps, energy, after):
    _, order, _ = sums.shape
    return pl.pallas_call(
        ordered(functools.partial(pair_body, energy), 4),
        in_specs=[WHOLE] * 4 + [ANYWHERE],
        out_specs=[WHOLE] * 2,
        out_shape=[jax.ShapeDtypeStruct((order, 2 * order), t) for t in (F32, BF16)],
        compiler_params=params(),
        cost_estimate=cost(),
        name="pair_sum",
    )(arrived, own, sums, maps, after)


def combine(arrived, maps, base, energy, after):
    count = len(arrived)

    def body(*refs):
        t_ref, base_ref, _, out = refs[count:]
        out[...] = (base_ref[...] + congruence(t_ref.at[energy], entered(refs[:count]))).astype(BF16)

    return pl.pallas_call(
        body,
        in_specs=[WHOLE] * (count + 2) + [ANYWHERE],
        out_specs=WHOLE,
        out_shape=jax.ShapeDtypeStruct(base.shape, BF16),
        compiler_params=params(),
        cost_estimate=cost(),
        name="combine",
    )(*arrived, maps, base, after)


def spread(maps, entry, sums, store):
    slabs, order, _ = sums.shape
    rows = maps[...].reshape(slabs * 2 * order, 2 * order)
    both = dot(rows, panel(entry[:, :order], entry[:, order:]))
    for s in range(slabs):
        first = 2 * s * order
        inner = both[first : first + order] + both[first + order : first + 2 * order]
        store(s, times_adjoint(inner, maps[s, 0], maps[s, 1]) + sums[s])


def from_partner(before_ref):
    odd = (lax.axis_index("slab") & 1) == 1
    return jnp.where(odd, before_ref[...], jnp.zeros_like(before_ref))


def entry_maps(prefixes, inner, energy, after):
    _, slabs, _, order, _ = prefixes.shape

    def body(p_ref, i_ref, _, out):
        high, low = panels(i_ref.at[energy])
        ih = panel(high[:, :order], high[:, order:])
        il = panel(low[:, :order], low[:, order:])
        for s in range(slabs):
            both = dot(p_ref[energy, s].reshape(2 * order, 2 * order), ih)
            store_map(out.at[0, s], both[:order] + both[order:] + dot(p_ref[energy, s, 0], il))

    return pl.pallas_call(
        body,
        in_specs=[WHOLE] * 2 + [ANYWHERE],
        out_specs=WHOLE,
        out_shape=jax.ShapeDtypeStruct((1,) + prefixes.shape[1:], BF16),
        compiler_params=params(),
        cost_estimate=cost(),
        name="entry_maps",
    )(prefixes, inner, after)


def part_known(before, prefixes, sums, energy, after):
    def body(before_ref, p_ref, sum_ref, _, out):
        def store(s, value):
            out[s] = value

        spread(p_ref.at[energy], from_partner(before_ref), sum_ref, store)

    return pl.pallas_call(
        body,
        in_specs=[WHOLE] * 3 + [ANYWHERE],
        out_specs=WHOLE,
        out_shape=jax.ShapeDtypeStruct(sums.shape, F32),
        compiler_params=params(),
        cost_estimate=cost(),
        name="part_known",
    )(before, prefixes, sums, after)


def finish_body(energy, maps_index, arrivals, before, m_ref, base_ref, out, blocks, sems):
    order = base_ref.shape[1]
    entry = entered(arrivals)
    if before is not None:
        before_ref, t_ref = before
        whole = from_partner(before_ref).astype(F32) + congruence(t_ref.at[energy], entry)
        entry = whole.astype(BF16)
    copies = []

    def store(s, value):
        blocks[s, 0] = value[:, :order]
        blocks[s, 1] = value[:, order:]
        copies.append(pltpu.make_async_copy(blocks.at[s], out.at[:, energy, s], sems.at[s]))
        copies[-1].start()

    spread(m_ref.at[maps_index], entry, base_ref, store)
    for copy in copies:
        copy.wait()


def finish(arrived, before, maps, maps_index, sums, energy, energies, held, after):
    slabs, order, _ = sums.shape
    count = len(arrived)
    extra = [] if before is None else list(before)
    operands = list(arrived) + extra + [maps, sums]
    in_specs = [WHOLE] * len(operands) + [ANYWHERE]
    operands.append(after)
    aliases = {}
    if held is not None:
        aliases = {len(operands): 0}
        operands.append(held)
        in_specs.append(ANYWHERE)

    def body(*refs):
        second = count + len(extra)
        finish_body(
            energy,
            maps_index,
            refs[:count],
            refs[count:second] if extra else None,
            *refs[second : second + 2],
            *refs[-3:],
        )

    return pl.pallas_call(
        body,
        in_specs=in_specs,
        out_specs=ANYWHERE,
        out_shape=jax.ShapeDtypeStruct((2, energies, slabs, order, order), F32),
        input_output_aliases=aliases,
        scratch_shapes=[pltpu.VMEM((slabs, 2, order, order), F32), pltpu.SemaphoreType.DMA((slabs,))],
        compiler_params=params(),
        cost_estimate=cost(),
        name="finish",
    )(*operands)


def swap(x, k):
    count = lax.axis_size("energy")
    return lax.ppermute(x, "energy", [(i, i ^ k) for i in range(count)])


def other_of_pair(x):
    return lax.ppermute(x, "slab", [(i, i ^ 1) for i in range(lax.axis_size("slab"))])


def forward(x, pair):
    return lax.ppermute(x, "slab", [(2 * pair + i, 2 * pair + 2 + i) for i in range(2)])


def cut(slabs):
    return [(0, slabs - 1), (slabs - 1, 1)] if slabs > 1 else [(0, slabs)]


def per_device(green_lesser, screened_lesser, green_retarded, coupling):
    count = lax.axis_size("energy")
    depth = lax.axis_size("slab")
    if depth % 2 or count & (count - 1):
        raise ValueError("mesh axes")
    _, energies, slabs, order, _ = green_lesser.shape
    far = [k for k in range(count) if k >= 2]
    near = [k for k in range(min(2, count))]
    parts = cut(slabs)

    def first_rows(k, start, size):
        rows = order // count
        begin = (0, 0, start, (lax.axis_index("energy") ^ k) * rows, 0)
        sizes = (2, energies, size, rows, order)
        return [lax.dynamic_slice(x, begin, sizes) for x in (green_lesser, screened_lesser)]

    pieces = [[None] * count for _ in parts]
    places = [(chunk, k) for chunk in range(len(parts)) for k in far + near]
    chunk, k = places[0]
    token = jnp.stack(first_rows(k, *parts[chunk]))
    pieces[chunk][k] = swap(token, k) if k else token
    urgent = [place for place in places[1:] if place[0] == 0 and place[1]]
    for group in (urgent, [place for place in places[1:] if place not in urgent]):
        if group:
            packed = pack(green_lesser, screened_lesser, [(k,) + parts[chunk] for chunk, k in group], count, token)
            for (chunk, k), block in zip(group, packed):
                pieces[chunk][k] = swap(block, k) if k else block
            token = packed[0]

    kernels, prefixes = build_maps(green_retarded, coupling, token)
    token = kernels
    mine = [prefixes[e, slabs - 1] for e in range(energies)]
    other = [other_of_pair(x) for x in mine]

    blocks = ()
    for chunk, (start, size) in enumerate(parts):
        if chunk == len(parts) - 1:
            pair_step, plane, inner = pair_maps(mine, other, energies, token)
            token = plane
        blocks = convolve(pieces[chunk], start, slabs, size, blocks, token)
        token = blocks[0]
    sigma = [[None] * count for _ in range(energies)]
    for e in range(energies):
        for k in range(count):
            block = blocks[k * energies + e]
            sigma[e][k] = swap(block, k) if k else block

    pairs = depth // 2
    final = energies - 1
    entries = token = entry_maps(prefixes, inner, final, token)
    known = None
    sums, own, ours = ([None] * energies for _ in range(3))
    running, carry = [None] * energies, [None] * energies
    arrived = [[] for _ in range(energies)]

    def stage(e, step):
        nonlocal token
        if step == 0:
            sums[e], own[e] = build_sources(sigma[e], green_retarded, kernels, e, token)
            token = own[e]
            ours[e] = other_of_pair(own[e])
        elif step == 1:
            running[e], carry[e] = pair_sum(ours[e], own[e], sums[e], pair_step, e, token)
            token = carry[e]
            arrived[e].append(forward(carry[e], 0))
        else:
            carry[e] = token = combine(arrived[e], plane, running[e], e, token)
            arrived[e].append(forward(carry[e], step - 1))

    last = max(pairs - 1, 1)
    for step in range(last + 1):
        for e in range(energies):
            stage(e, step)
        if step == min(2, last):
            known = token = part_known(ours[final], prefixes, sums[final], final, token)
    result = None
    for e in range(final):
        result = finish(
            arrived[e], (ours[e], inner), prefixes, e, sums[e], e, energies, result, token
        )
    return finish(arrived[final], None, entries, 0, known, final, energies, result, token)


def solution(mesh):
    placed = (
        P(None, "energy", "slab", None, None),
        P(None, "energy", "slab", None, None),
        P(None, "energy", "slab", None, None),
        P(None, "slab", None, None),
    )
    return jax.shard_map(
        per_device,
        mesh=mesh,
        in_specs=placed,
        out_specs=P(None, "energy", "slab", None, None),
        check_vma=False,
    )
```

```python
import functools

import jax
import jax.numpy as jnp
from jax import lax
from jax.experimental import pallas as pl
from jax.experimental.pallas import tpu as pltpu
from jax.sharding import PartitionSpec as P

BF16 = jnp.bfloat16
F32 = jnp.float32
VMEM_LIMIT = 36 * 1024 * 1024


def params():
    return pltpu.CompilerParams(vmem_limit_bytes=VMEM_LIMIT)


def ordered(body, count, extra=1):
    def run(*refs):
        body(*refs[:count], *refs[count + extra :])

    return run


ANYWHERE = pl.BlockSpec(memory_space=pl.ANY)
WHOLE = pl.BlockSpec(memory_space=pltpu.VMEM)


def cost():
    return pl.CostEstimate(flops=0, bytes_accessed=0, transcendentals=0)


def split(value):
    high = value.astype(BF16)
    low = (value - high.astype(F32)).astype(BF16)
    return high, low


def panel(re, im):
    return jnp.concatenate(
        [jnp.concatenate([re, im], axis=1), jnp.concatenate([-im, re], axis=1)], axis=0
    )


def dot(left, right):
    return lax.dot_general(left, right, (((1,), (0,)), ((), ())), preferred_element_type=F32)


def dot_nt(left, right):
    return lax.dot_general(left, right, (((1,), (1,)), ((), ())), preferred_element_type=F32)


def times_wide(a_high, a_low, x):
    order = x.shape[0]
    x_high, x_low = split(x)
    both = dot(jnp.concatenate([a_high, a_low], axis=0), panel(x_high[:, :order], x_high[:, order:]))
    return both[:order] + both[order:] + dot(a_high, panel(x_low[:, :order], x_low[:, order:]))


def times_narrow(a_high, a_low, re, im):
    order = re.shape[0]
    both = dot(jnp.concatenate([a_high, a_low], axis=0), panel(re, im))
    return both[:order] + both[order:]


def times_adjoint(y, t_high, t_low):
    order = y.shape[0]
    y_high, y_low = split(y)
    th = panel(t_high[:, :order], t_high[:, order:])
    tl = panel(t_low[:, :order], t_low[:, order:])
    both = dot_nt(jnp.concatenate([y_high, y_low], axis=0), th)
    return both[:order] + both[order:] + dot_nt(y_high, tl)


def panels(ref):
    return ref[0], ref[1]


def store_map(ref, value):
    high, low = split(value)
    ref[0] = high
    ref[1] = low


def pack_body(wanted, *refs):
    sources, outs, sems = refs[:2], refs[-1 - len(wanted) : -1], refs[-1]
    copies = []
    for out, (k, start) in zip(outs, wanted):
        size, rows = out.shape[3:5]
        begin = pl.multiple_of((lax.axis_index("energy") ^ k) * rows, rows)
        for part in range(2):
            block = sources[part].at[:, :, pl.ds(start, size), pl.ds(begin, rows), :]
            copies.append(pltpu.make_async_copy(block, out.at[part], sems.at[len(copies)]))
    for copy in copies:
        copy.start()
    for copy in copies:
        copy.wait()


def pack(green, screen, wanted, count, after):
    _, energies, _, order, _ = green.shape
    return pl.pallas_call(
        functools.partial(pack_body, [w[:2] for w in wanted]),
        in_specs=[ANYWHERE] * 3,
        out_specs=[WHOLE] * len(wanted),
        out_shape=[
            jax.ShapeDtypeStruct((2, 2, energies, size, order // count, order), BF16) for _, _, size in wanted
        ],
        scratch_shapes=[pltpu.SemaphoreType.DMA((2 * len(wanted),))],
        compiler_params=params(),
        cost_estimate=cost(),
        name="pack",
    )(green, screen, after)


def maps_body(g_ref, c_ref, k_ref, p_ref, carry):
    left = jnp.concatenate([g_ref[0], g_ref[1]], axis=1)
    value = dot(left, panel(c_ref[0], c_ref[1]))
    store_map(k_ref, value)

    @pl.when(pl.program_id(1) == 0)
    def _():
        carry[...] = value

    @pl.when(pl.program_id(1) > 0)
    def _():
        high, low = panels(k_ref)
        carry[...] = times_wide(high, low, carry[...])

    store_map(p_ref, carry[...])


def build_maps(green, coupling, *after):
    _, energies, slabs, order, _ = green.shape
    shape = jax.ShapeDtypeStruct((energies, slabs, 2, order, 2 * order), BF16)
    out_spec = pl.BlockSpec((None, None, 2, order, 2 * order), lambda e, s: (e, s, 0, 0, 0))
    return pl.pallas_call(
        lambda *refs: maps_body(*refs[:2], *refs[2 + len(after) :]),
        grid=(energies, slabs),
        in_specs=[
            pl.BlockSpec((2, None, None, order, order), lambda e, s: (0, e, s, 0, 0)),
            pl.BlockSpec((2, None, order, order), lambda e, s: (0, s, 0, 0)),
        ]
        + [ANYWHERE] * len(after),
        out_specs=[out_spec, out_spec],
        out_shape=[shape, shape],
        scratch_shapes=[pltpu.VMEM((order, 2 * order), F32)],
        compiler_params=params(),
        cost_estimate=cost(),
        name="maps",
    )(green, coupling, *after)


def one_map(maps, energy):
    if isinstance(maps, list):
        return maps[energy], pl.BlockSpec(maps[energy].shape, lambda *_: (0, 0, 0))
    return maps, pl.BlockSpec((None,) + maps.shape[1:], lambda *_: (energy, 0, 0, 0))


def pair_maps_body(energies, *refs):
    step, plane, inner = refs[-3:]
    odd = (lax.axis_index("slab") & 1) == 1
    for e in range(energies):
        mine, other = refs[2 * e], refs[2 * e + 1]
        order = mine.shape[1]
        first = [jnp.where(odd, mine[part], other[part]) for part in range(2)]
        second = [jnp.where(odd, other[part], mine[part]).astype(F32) for part in range(2)]
        store_map(plane.at[e], times_wide(*first, second[0] + second[1]))
        row = lax.broadcasted_iota(jnp.int32, (order, 2 * order), 0)
        column = lax.broadcasted_iota(jnp.int32, (order, 2 * order), 1)
        unit = jnp.where(row == column, 1.0, 0.0)
        for part in range(2):
            step[e, part] = first[part]
            identity = unit if part == 0 else jnp.zeros_like(unit)
            inner[e, part] = jnp.where(odd, other[part].astype(F32), identity).astype(BF16)


def pair_maps(mine, other, energies, after):
    pairs = [one_map(maps, e) for e in range(energies) for maps in (mine, other)]
    shape = (energies,) + pairs[0][1].block_shape[-3:]
    return pl.pallas_call(
        ordered(functools.partial(pair_maps_body, energies), 2 * energies),
        grid=(1,),
        in_specs=[spec for _, spec in pairs] + [ANYWHERE],
        out_specs=[pl.BlockSpec(shape, lambda i: (0, 0, 0, 0))] * 3,
        out_shape=[jax.ShapeDtypeStruct(shape, BF16)] * 3,
        compiler_params=params(),
        cost_estimate=cost(),
        name="pair_maps",
    )(*[maps for maps, _ in pairs], after)


def convolve_body(pairs, energies, shared, *refs):
    count = len(pairs)
    taken = sum(1 + pair for pair in pairs)
    ins, outs = list(refs[:taken]), refs[taken + 1 + shared :]
    green, screen, total = refs[-3:]
    me = lax.axis_index("energy")
    points = count * energies
    middle = points // 2
    share = 1.0 / points
    rows, columns = green.shape[2:]
    for k in range(count):
        base = (me ^ k) * energies
        piece = ins.pop(0)
        halves = (piece, ins.pop(0)) if pairs[k] else (piece.at[0], piece.at[1])
        for e in range(energies):
            green[:, base + e] = halves[0][:, e].astype(F32)
            screen[:, base + e] = halves[1][:, e].astype(F32)

    def tile(index, _):
        row = pl.multiple_of(index * 8, 8)
        for col in range(0, columns, 128):
            at = (pl.ds(row, 8), pl.ds(col, 128))
            gr = [green[(0, m) + at] for m in range(points)]
            gi = [green[(1, m) + at] for m in range(points)]
            wr = [screen[(0, m) + at] for m in range(points)]
            wi = [screen[(1, m) + at] for m in range(points)]
            for n in range(points):
                re = None
                im = None
                for m in range(points):
                    lag = n - m + middle
                    if 0 <= lag < points:
                        a = gr[m] * wr[lag] - gi[m] * wi[lag]
                        b = gr[m] * wi[lag] + gi[m] * wr[lag]
                        re = a if re is None else re + a
                        im = b if im is None else im + b
                total[(n, 0) + at] = im * -share
                total[(n, 1) + at] = re * share
        return 0

    lax.fori_loop(0, rows // 8, tile, 0)
    for k in range(count):
        base = (me ^ k) * energies
        for e in range(energies):
            outs[k * energies + e][...] = total[base + e].astype(BF16)


def convolve(pieces, start, slabs, size, held, after):
    count = len(pieces)
    pairs = [isinstance(piece, tuple) for piece in pieces]
    operands, in_specs = [], []
    for piece, pair in zip(pieces, pairs):
        if pair:
            operands += piece
            energies, _, rows, columns = piece[0].shape[1:]
            in_specs += [pl.BlockSpec((2, energies, None, rows, columns), lambda s: (0, 0, s + start, 0, 0))] * 2
        else:
            operands.append(piece)
            energies, _, rows, columns = piece.shape[2:]
            first = start if piece.shape[3] == slabs else 0
            block = (2, 2, energies, None, rows, columns)
            in_specs.append(pl.BlockSpec(block, lambda s, first=first: (0, 0, 0, s + first, 0, 0)))
    points = count * energies
    whole = pl.BlockSpec((None, 2, rows, columns), lambda s: (s + start, 0, 0, 0))
    outs = pl.pallas_call(
        functools.partial(convolve_body, pairs, energies, len(held)),
        grid=(size,),
        in_specs=in_specs + [ANYWHERE] * (1 + len(held)),
        out_specs=[whole] * points,
        out_shape=[jax.ShapeDtypeStruct((slabs, 2, rows, columns), BF16)] * points,
        input_output_aliases={len(operands) + 1 + i: i for i in range(len(held))},
        scratch_shapes=[
            pltpu.VMEM((2, points, rows, columns), F32),
            pltpu.VMEM((2, points, rows, columns), F32),
            pltpu.VMEM((points, 2, rows, columns), F32),
        ],
        compiler_params=params(),
        cost_estimate=cost(),
        name="convolve",
    )(*operands, after, *held)
    return outs


def source_body(energy, owners, *refs):
    pieces = refs[: len(owners)]
    g_ref, k_ref, b_ref, v_ref, sigma = refs[len(owners) :]
    me = lax.axis_index("energy")
    for piece, k in zip(pieces, owners):
        slabs, _, rows, _ = piece.shape
        start = pl.multiple_of((me ^ k) * rows, rows)
        for s in range(slabs):
            for part in range(2):
                sigma[s, part, pl.ds(start, rows), :] = piece[s, part]

    carry = None
    for s in range(sigma.shape[0]):
        green_re, green_im = g_ref[0, energy, s], g_ref[1, energy, s]
        left = jnp.concatenate([green_re, green_im], axis=1)
        mixed = dot(left, panel(sigma[s, 0], sigma[s, 1])).astype(BF16)
        source = dot_nt(mixed, panel(green_re, green_im))
        if carry is not None:
            high, low = k_ref[energy, s, 0], k_ref[energy, s, 1]
            source = times_adjoint(times_wide(high, low, carry), high, low) + source
        carry = source
        b_ref[s] = carry
    v_ref[...] = carry.astype(BF16)


def build_sources(pieces, green, kernels, energy, after):
    slabs, order = green.shape[2:4]
    owners = [k for k in range(len(pieces)) if k >= 2] + [k for k in (1, 0) if k < len(pieces)]
    pieces = [pieces[k] for k in owners]
    return pl.pallas_call(
        ordered(functools.partial(source_body, energy, owners), len(pieces) + 2),
        in_specs=[WHOLE] * (len(pieces) + 2) + [ANYWHERE],
        out_specs=[WHOLE] * 2,
        out_shape=[
            jax.ShapeDtypeStruct((slabs, order, 2 * order), F32),
            jax.ShapeDtypeStruct((order, 2 * order), BF16),
        ],
        scratch_shapes=[pltpu.VMEM((slabs, 2, order, order), BF16)],
        compiler_params=params(),
        cost_estimate=cost(),
        name="sources",
    )(*pieces, green, kernels, after)


def congruence(t_ref, x):
    order = x.shape[0]
    high, low = panels(t_ref)
    if x.dtype == F32:
        inner = times_wide(high, low, x)
    else:
        inner = times_narrow(high, low, x[:, :order], x[:, order:])
    return times_adjoint(inner, high, low)


def entered(refs):
    pair = lax.axis_index("slab") >> 1
    value = jnp.zeros(refs[0].shape, refs[0].dtype)
    for step, ref in enumerate(refs):
        value = jnp.where(pair == step + 1, ref[...], value)
    return value


def pair_body(energy, v_ref, own_ref, sum_ref, t_ref, full_ref, short_ref):
    odd = (lax.axis_index("slab") & 1) == 1
    theirs = v_ref[...]
    x = jnp.where(odd, theirs, own_ref[...])
    base = jnp.where(odd, sum_ref[sum_ref.shape[0] - 1], theirs.astype(F32))
    value = base + congruence(t_ref.at[energy], x)
    full_ref[...] = value
    short_ref[...] = value.astype(BF16)


def pair_sum(arrived, own, sums, maps, energy, after):
    _, order, _ = sums.shape
    return pl.pallas_call(
        ordered(functools.partial(pair_body, energy), 4),
        in_specs=[WHOLE] * 4 + [ANYWHERE],
        out_specs=[WHOLE] * 2,
        out_shape=[jax.ShapeDtypeStruct((order, 2 * order), t) for t in (F32, BF16)],
        compiler_params=params(),
        cost_estimate=cost(),
        name="pair_sum",
    )(arrived, own, sums, maps, after)


def combine(arrived, maps, base, energy, after):
    count = len(arrived)

    def body(*refs):
        t_ref, base_ref, _, out = refs[count:]
        out[...] = (base_ref[...] + congruence(t_ref.at[energy], entered(refs[:count]))).astype(BF16)

    return pl.pallas_call(
        body,
        in_specs=[WHOLE] * (count + 2) + [ANYWHERE],
        out_specs=WHOLE,
        out_shape=jax.ShapeDtypeStruct(base.shape, BF16),
        compiler_params=params(),
        cost_estimate=cost(),
        name="combine",
    )(*arrived, maps, base, after)


def spread(maps, entry, sums, store):
    slabs, order, _ = sums.shape
    rows = maps[...].reshape(slabs * 2 * order, 2 * order)
    both = dot(rows, panel(entry[:, :order], entry[:, order:]))
    for s in range(slabs):
        first = 2 * s * order
        inner = both[first : first + order] + both[first + order : first + 2 * order]
        store(s, times_adjoint(inner, maps[s, 0], maps[s, 1]) + sums[s])


def from_partner(before_ref):
    odd = (lax.axis_index("slab") & 1) == 1
    return jnp.where(odd, before_ref[...], jnp.zeros_like(before_ref))


def entry_maps(prefixes, inner, energy, after):
    _, slabs, _, order, _ = prefixes.shape

    def body(p_ref, i_ref, _, out):
        high, low = panels(i_ref.at[energy])
        ih = panel(high[:, :order], high[:, order:])
        il = panel(low[:, :order], low[:, order:])
        for s in range(slabs):
            both = dot(p_ref[energy, s].reshape(2 * order, 2 * order), ih)
            store_map(out.at[0, s], both[:order] + both[order:] + dot(p_ref[energy, s, 0], il))

    return pl.pallas_call(
        body,
        in_specs=[WHOLE] * 2 + [ANYWHERE],
        out_specs=WHOLE,
        out_shape=jax.ShapeDtypeStruct((1,) + prefixes.shape[1:], BF16),
        compiler_params=params(),
        cost_estimate=cost(),
        name="entry_maps",
    )(prefixes, inner, after)


def part_known(before, prefixes, sums, energy, after):
    def body(before_ref, p_ref, sum_ref, _, out):
        def store(s, value):
            out[s] = value

        spread(p_ref.at[energy], from_partner(before_ref), sum_ref, store)

    return pl.pallas_call(
        body,
        in_specs=[WHOLE] * 3 + [ANYWHERE],
        out_specs=WHOLE,
        out_shape=jax.ShapeDtypeStruct(sums.shape, F32),
        compiler_params=params(),
        cost_estimate=cost(),
        name="part_known",
    )(before, prefixes, sums, after)


def finish_body(energy, maps_index, arrivals, before, m_ref, base_ref, out, blocks, sems):
    order = base_ref.shape[1]
    entry = entered(arrivals)
    if before is not None:
        before_ref, t_ref = before
        whole = from_partner(before_ref).astype(F32) + congruence(t_ref.at[energy], entry)
        entry = whole.astype(BF16)
    copies = []

    def store(s, value):
        blocks[s, 0] = value[:, :order]
        blocks[s, 1] = value[:, order:]
        copies.append(pltpu.make_async_copy(blocks.at[s], out.at[:, energy, s], sems.at[s]))
        copies[-1].start()

    spread(m_ref.at[maps_index], entry, base_ref, store)
    for copy in copies:
        copy.wait()


def finish(arrived, before, maps, maps_index, sums, energy, energies, held, after):
    slabs, order, _ = sums.shape
    count = len(arrived)
    extra = [] if before is None else list(before)
    operands = list(arrived) + extra + [maps, sums]
    in_specs = [WHOLE] * len(operands) + [ANYWHERE]
    operands.append(after)
    aliases = {}
    if held is not None:
        aliases = {len(operands): 0}
        operands.append(held)
        in_specs.append(ANYWHERE)

    def body(*refs):
        second = count + len(extra)
        finish_body(
            energy,
            maps_index,
            refs[:count],
            refs[count:second] if extra else None,
            *refs[second : second + 2],
            *refs[-3:],
        )

    return pl.pallas_call(
        body,
        in_specs=in_specs,
        out_specs=ANYWHERE,
        out_shape=jax.ShapeDtypeStruct((2, energies, slabs, order, order), F32),
        input_output_aliases=aliases,
        scratch_shapes=[pltpu.VMEM((slabs, 2, order, order), F32), pltpu.SemaphoreType.DMA((slabs,))],
        compiler_params=params(),
        cost_estimate=cost(),
        name="finish",
    )(*operands)


def swap(x, k):
    count = lax.axis_size("energy")
    return lax.ppermute(x, "energy", [(i, i ^ k) for i in range(count)])


def other_of_pair(x):
    return lax.ppermute(x, "slab", [(i, i ^ 1) for i in range(lax.axis_size("slab"))])


def forward(x, pair):
    return lax.ppermute(x, "slab", [(2 * pair + i, 2 * pair + 2 + i) for i in range(2)])


def cut(slabs):
    return [(0, slabs - 1), (slabs - 1, 1)] if slabs > 1 else [(0, slabs)]


def per_device(green_lesser, screened_lesser, green_retarded, coupling):
    count = lax.axis_size("energy")
    depth = lax.axis_size("slab")
    if depth % 2 or count & (count - 1):
        raise ValueError("mesh axes")
    _, energies, slabs, order, _ = green_lesser.shape
    far = [k for k in range(count) if k >= 2]
    near = [k for k in range(min(2, count))]
    parts = cut(slabs)

    def first_rows(k, start, size):
        rows = order // count
        begin = (0, 0, start, (lax.axis_index("energy") ^ k) * rows, 0)
        sizes = (2, energies, size, rows, order)
        return [lax.dynamic_slice(x, begin, sizes) for x in (green_lesser, screened_lesser)]

    pieces = [[None] * count for _ in parts]
    places = [(chunk, k) for chunk in range(len(parts)) for k in far + near]
    chunk, k = places[0]
    token = jnp.stack(first_rows(k, *parts[chunk]))
    pieces[chunk][k] = swap(token, k) if k else token
    urgent = [place for place in places[1:] if place[0] == 0 and place[1]]
    for group in (urgent, [place for place in places[1:] if place not in urgent]):
        if group:
            packed = pack(green_lesser, screened_lesser, [(k,) + parts[chunk] for chunk, k in group], count, token)
            for (chunk, k), block in zip(group, packed):
                pieces[chunk][k] = swap(block, k) if k else block
            token = packed[0]

    kernels, prefixes = build_maps(green_retarded, coupling, token)
    token = kernels
    mine = [prefixes[e, slabs - 1] for e in range(energies)]
    other = [other_of_pair(x) for x in mine]

    blocks = ()
    for chunk, (start, size) in enumerate(parts):
        if chunk == len(parts) - 1:
            pair_step, plane, inner = pair_maps(mine, other, energies, token)
            token = plane
        blocks = convolve(pieces[chunk], start, slabs, size, blocks, token)
        token = blocks[0]
    sigma = [[None] * count for _ in range(energies)]
    for e in range(energies):
        for k in range(count):
            block = blocks[k * energies + e]
            sigma[e][k] = swap(block, k) if k else block

    pairs = depth // 2
    final = energies - 1
    entries = token = entry_maps(prefixes, inner, final, token)
    known = None
    sums, own, ours = ([None] * energies for _ in range(3))
    running, carry = [None] * energies, [None] * energies
    arrived = [[] for _ in range(energies)]

    def stage(e, step):
        nonlocal token
        if step == 0:
            sums[e], own[e] = build_sources(sigma[e], green_retarded, kernels, e, token)
            token = own[e]
            ours[e] = other_of_pair(own[e])
        elif step == 1:
            running[e], carry[e] = pair_sum(ours[e], own[e], sums[e], pair_step, e, token)
            token = carry[e]
            arrived[e].append(forward(carry[e], 0))
        else:
            carry[e] = token = combine(arrived[e], plane, running[e], e, token)
            arrived[e].append(forward(carry[e], step - 1))

    last = max(pairs - 1, 1)
    for step in range(last + 1):
        for e in range(energies):
            stage(e, step)
        if step == min(2, last):
            known = token = part_known(ours[final], prefixes, sums[final], final, token)
    result = None
    for e in range(final):
        result = finish(
            arrived[e], (ours[e], inner), prefixes, e, sums[e], e, energies, result, token
        )
    return finish(arrived[final], None, entries, 0, known, final, energies, result, token)


def solution(mesh):
    placed = (
        P(None, "energy", "slab", None, None),
        P(None, "energy", "slab", None, None),
        P(None, "energy", "slab", None, None),
        P(None, "slab", None, None),
    )
    return jax.shard_map(
        per_device,
        mesh=mesh,
        in_specs=placed,
        out_specs=P(None, "energy", "slab", None, None),
        check_vma=False,
    )
```
